32 devices in a mesh: rows: 4 (over x, core), cols: 8 (over z, y).
Axes of the slice: x: 2, y: 2, z: 4, core: 2. Of those that a mesh axis runs over, the one named last changes fastest.
Arguments:
- tokens: bfloat16 [8192, 2048], P('rows', 'cols'), may hold values from -6 to 6
- segment_ids: int32 [4, 2048], P('rows'), may hold values from 0 to 7, never falling along the last dimension, each value on 1 to 1024 neighbouring positions
- w_query: bfloat16 [2048, 2048], P('rows', 'cols'), may hold values from -0.125 to 0.125
- w_key: bfloat16 [2048, 2048], P('rows', 'cols'), may hold values from -0.125 to 0.125
- w_value: bfloat16 [2048, 2048], P('rows', 'cols'), may hold values from -0.125 to 0.125
- w_out: bfloat16 [2048, 2048], P('cols', 'rows'), may hold values from -0.125 to 0.125
- w_gate: bfloat16 [2048, 8192], P('rows', 'cols'), may hold values from -0.125 to 0.125
- w_up: bfloat16 [2048, 8192], P('rows', 'cols'), may hold values from -0.125 to 0.125
- w_down: bfloat16 [8192, 2048], P('cols', 'rows'), may hold values from -0.0625 to 0.0625
- q_gain: float32 [2048], P('cols'), may hold values from 0.1 to 1.9
- k_gain: float32 [2048], P('cols'), may hold values from 0.1 to 1.9
- attn_gain: float32 [2048], P('cols'), may hold values from 0.1 to 1.9
- ffn_gain: float32 [2048], P('cols'), may hold values from 0.1 to 1.9
- out_grad: bfloat16 [8192, 2048], P('rows', 'cols'), may hold values from -6 to 6
Outputs:
- layer_out: bfloat16 [8192, 2048], P('rows', 'cols')
- input_grad: bfloat16 [8192, 2048], P('rows', 'cols')
- grad_query: float32 [2048, 2048], P('rows', 'cols')
- grad_key: float32 [2048, 2048], P('rows', 'cols')
- grad_value: float32 [2048, 2048], P('rows', 'cols')
- grad_out: float32 [2048, 2048], P('cols', 'rows')
- grad_gate: float32 [2048, 8192], P('rows', 'cols')
- grad_up: float32 [2048, 8192], P('rows', 'cols')
- grad_down: float32 [8192, 2048], P('cols', 'rows')
- grad_q_gain: float32 [2048], P('cols')
- grad_k_gain: float32 [2048], P('cols')
- grad_attn_gain: float32 [2048], P('cols')
- grad_ffn_gain: float32 [2048], P('cols')
The draws below stay inside these ranges and needn't reach their ends.
Inputs may be any that keep to these rules, and one draw needn't show every extreme that they name: `segment_ids`: within a sequence the ids never fall; every id from 0 to 7 is used and names 1 to 1024 consecutive tokens.
All inputs are finite; a program needn't handle non-finite values.
Results may differ from the reference program's by a relative error of at most 0.019.
Values may be sent and summed in bfloat16 or wider, within the bound.
No kernel may reach another device: no remote copies, remote signals or barrier semaphores. Data moves between devices by JAX's collectives and lax.ppermute only.
A program may use at most 256 MiB of HBM per device.

```python
import math
import jax
import jax.numpy as jnp
import numpy as np
from jax import lax

D = 2048
HEADS = 16
HEAD_DIM = 128
FF = 8192
SEQ = 2048
SEQS = 4
TOKENS = 8192
SEGS = 8
DOC_MOST = 1024


def shard_levels(stream_key, shape, split, low, top_value):
    def one(dim, shards_of):
        draws = jax.random.uniform(jax.random.fold_in(jax.random.fold_in(stream_key, 6), dim), (shards_of,), jnp.float32, low / len(split), top_value / len(split))
        return jnp.repeat(jnp.exp(draws), shape[dim] // shards_of).reshape((-1,) + (1,) * (len(shape) - dim - 1))

    level = one(*split[0])
    for cut in split[1:]:
        level = level * one(*cut)
    return level


def split_up(count, total, most, skew):
    weights = [(1 << 20) // math.isqrt(rank ** skew) + 1 for rank in range(2, count + 1)]
    rest, holding = total - most - (count - 1), [1] * (count - 1)
    while rest > 0:
        free = [i for i in range(count - 1) if holding[i] < most]
        whole, remaining = sum([weights[i] for i in free]), rest
        for i in free:
            extra = min(most - holding[i], max(1, remaining * weights[i] // whole), rest)
            holding[i] = holding[i] + extra
            rest = rest - extra
    return np.array([most] + holding)


def uneven(own_key, amount, total, limit, lean):
    if amount == 2:
        one = jax.random.randint(own_key, (), max(1, total - limit), min(limit, total - 1) + 1)
        return jnp.stack([one, total - one])
    sizes = jnp.asarray(split_up(amount, total, limit, lean), jnp.int32)
    twos = (amount - 1) // 2
    giver, taker = sizes[1:1 + 2 * twos:2], sizes[2:2 + 2 * twos:2]
    slack = jnp.minimum(giver - 1, limit - taker)
    passed = jax.random.randint(jax.random.fold_in(own_key, 1), (twos,), 0, 1 << 20) % (slack + 1)
    sizes = sizes.at[1:1 + 2 * twos:2].set(giver - passed).at[2:2 + 2 * twos:2].set(taker + passed)
    return sizes[jax.random.permutation(jax.random.fold_in(own_key, 2), amount)]


def noise(key, dims, spread, bound, shards=(), held_as=jnp.bfloat16):
    entries = jax.random.normal(key, dims, jnp.float32) * spread
    if len(shards) > 0:
        entries = shard_levels(key, dims, shards, -0.22, 0.18) * entries
    return jnp.clip(entries, min=-bound, max=bound).astype(held_as)


def setup_inputs(seed: int = 0) -> dict:
    seeds = jax.random.split(jax.random.key(seed), 15)
    tokens = noise(seeds[0], (TOKENS, D), 1.0, 6.0, ((0, 4), (1, 8)))
    segment_ids = jax.vmap(lambda own: jnp.searchsorted(jnp.cumsum(uneven(own, SEGS, SEQ, DOC_MOST, 1)), jnp.arange(SEQ), side="right"))(jax.random.split(seeds[1], SEQS)).reshape((SEQS, SEQ)).astype(jnp.int32)
    w_query = noise(seeds[2], (D, D), D ** -0.5, 0.125, ((0, 4), (1, 8)))
    w_key = noise(seeds[3], (D, D), D ** -0.5, 0.125, ((0, 4), (1, 8)))
    w_value = noise(seeds[4], (D, D), D ** -0.5, 0.125, ((0, 4), (1, 8)))
    w_out = noise(seeds[5], (D, D), D ** -0.5, 0.125, ((0, 8), (1, 4)))
    w_gate = noise(seeds[6], (D, FF), D ** -0.5, 0.125, ((0, 4), (1, 8)))
    w_up = noise(seeds[7], (D, FF), D ** -0.5, 0.125, ((0, 4), (1, 8)))
    w_down = noise(seeds[8], (FF, D), FF ** -0.5, 0.0625, ((0, 8), (1, 4)))
    q_gain = jnp.clip(1.0 + 0.18 * jax.random.normal(seeds[9], (D,), jnp.float32), 0.1, 1.9)
    k_gain = jnp.clip(1.0 + 0.18 * jax.random.normal(seeds[10], (D,), jnp.float32), 0.1, 1.9)
    attn_gain = jnp.clip(1.0 + 0.18 * jax.random.normal(seeds[11], (D,), jnp.float32), 0.1, 1.9)
    ffn_gain = jnp.clip(1.0 + 0.18 * jax.random.normal(seeds[12], (D,), jnp.float32), 0.1, 1.9)
    out_grad = noise(seeds[13], (TOKENS, D), 1.0, 6.0, ((0, 4), (1, 8)))
    return dict(tokens=tokens, segment_ids=segment_ids, w_query=w_query, w_key=w_key, w_value=w_value, w_out=w_out, w_gate=w_gate, w_up=w_up, w_down=w_down, q_gain=q_gain, k_gain=k_gain, attn_gain=attn_gain, ffn_gain=ffn_gain, out_grad=out_grad)


EPS = 1e-06
THETA = 500000.0
HIGHEST = lax.Precision.HIGHEST

@jax.custom_vjp
def low(v):
    return lax.optimization_barrier(v.astype(jnp.bfloat16)).astype(jnp.float32)

@jax.custom_vjp
def low_back(v):
    return v

def low_keep(v):
    return (low(v), None)

def low_pass(kept, grad):
    return (grad,)

def back_keep(v):
    return (v, None)

def back_low(kept, grad):
    return (low(grad),)
low.defvjp(low_keep, low_pass)
low_back.defvjp(back_keep, back_low)

def matmul(left, right):
    return jnp.dot(left, right, precision=HIGHEST, preferred_element_type=jnp.float32)

def rms_scale(values):
    return lax.rsqrt(lax.optimization_barrier(jnp.mean(values * values, axis=-1, keepdims=True)) + EPS)

def rotary(values):
    halfway = values.shape[-1] // 2
    rates = THETA ** (-2.0 * jnp.arange(halfway, dtype=jnp.float32) / values.shape[-1])
    angles = jnp.arange(values.shape[-3], dtype=jnp.float32)[:, None] * rates[None, :]
    cosine = jnp.cos(angles)[:, None, :]
    sine_part = jnp.sin(angles)[:, None, :]
    former = values[..., :halfway]
    latter = values[..., halfway:]
    return jnp.concatenate([former * cosine - latter * sine_part, latter * cosine + former * sine_part], axis=-1)

def attend_sequence(packed):
    queries, keys_all, values_all, segment = packed
    length = queries.shape[0]
    block_rows = min(512, length)
    positions = jnp.arange(length, dtype=jnp.int32)

    def one_block(offset):
        block_query = lax.dynamic_slice_in_dim(queries, offset, block_rows, 0)
        block_seg = lax.dynamic_slice_in_dim(segment, offset, block_rows, 0)
        block_pos = offset + jnp.arange(block_rows, dtype=jnp.int32)
        scores = low_back(jnp.einsum('qhd,khd->hqk', block_query, keys_all, precision=HIGHEST))
        allowed = (block_seg[:, None] == segment[None, :]) & (positions[None, :] <= block_pos[:, None])
        scores = jnp.where(allowed[None], scores, -1e+30)
        row_max = lax.optimization_barrier(jnp.max(scores, axis=-1, keepdims=True))
        weights = jnp.exp(scores - row_max)
        weights = weights / lax.optimization_barrier(jnp.sum(weights, axis=-1, keepdims=True))
        return jnp.einsum('hqk,khd->qhd', low(weights), values_all, precision=HIGHEST)
    offsets = jnp.arange(0, length, block_rows, dtype=jnp.int32)
    blocks = lax.map(jax.checkpoint(one_block), offsets)
    return blocks.reshape(queries.shape)

def layer(segment_ids, tokens, w_query, w_key, w_value, w_out, w_gate, w_up, w_down, q_gain, k_gain, attn_gain, ffn_gain):
    shaped = (SEQS, SEQ, HEADS, HEAD_DIM)
    query_raw = low_back(matmul(tokens, w_query))
    key_raw = low_back(matmul(tokens, w_key))
    value_low = low(low_back(matmul(tokens, w_value)))
    query_normed = query_raw * rms_scale(query_raw) * q_gain
    key_normed = key_raw * rms_scale(key_raw) * k_gain
    query_low = low(rotary(query_normed.reshape(shaped)) * HEAD_DIM ** (-0.5))
    key_low = low(rotary(key_normed.reshape(shaped)))
    attended = lax.map(attend_sequence, (query_low, key_low, value_low.reshape(shaped), segment_ids))
    attn_low = low(low_back(attended.reshape(TOKENS, D)))
    attn_sum = low_back(matmul(attn_low, w_out))
    hidden = tokens + attn_sum * rms_scale(attn_sum) * attn_gain
    hidden_low = low(hidden)
    gate = low_back(matmul(hidden_low, w_gate))
    upward = low_back(matmul(hidden_low, w_up))
    mixed_low = low(jax.nn.silu(gate) * upward)
    ffn_sum = low_back(matmul(mixed_low, w_down))
    return hidden + ffn_sum * rms_scale(ffn_sum) * ffn_gain

def reference(tokens, segment_ids, w_query, w_key, w_value, w_out, w_gate, w_up, w_down, q_gain, k_gain, attn_gain, ffn_gain, out_grad):
    floats = (tokens.astype(jnp.float32), w_query.astype(jnp.float32), w_key.astype(jnp.float32), w_value.astype(jnp.float32), w_out.astype(jnp.float32), w_gate.astype(jnp.float32), w_up.astype(jnp.float32), w_down.astype(jnp.float32), q_gain.astype(jnp.float32), k_gain.astype(jnp.float32), attn_gain.astype(jnp.float32), ffn_gain.astype(jnp.float32))

    def forward(*inputs):
        return layer(segment_ids, *inputs)
    result, pullback = jax.vjp(forward, *floats)
    grads = pullback(out_grad.astype(jnp.float32))
    return (result.astype(jnp.bfloat16), grads[0].astype(jnp.bfloat16), grads[1], grads[2], grads[3], grads[4], grads[5], grads[6], grads[7], grads[8], grads[9], grads[10], grads[11])
```

```python
import functools

import jax
import jax.numpy as jnp
from jax import lax
from jax.experimental import pallas as pl
from jax.experimental.pallas import tpu as pltpu
from jax.sharding import PartitionSpec as P

HEAD_DIM = 128
EPS = 1e-06
THETA = 500000.0
MASKED = -1e30
LOW = jnp.bfloat16
WIDE = jnp.float32
CHUNKS = 4
DOCUMENTS = 8
VMEM = 52 * 2**20


def rotation(length, width):
    halfway = width // 2
    rates = THETA ** (-2.0 * jnp.arange(halfway, dtype=WIDE) / width)
    angles = jnp.arange(length, dtype=WIDE)[:, None] * rates[None, :]
    cosine, sine_part = jnp.cos(angles), jnp.sin(angles)
    return (
        jnp.concatenate([cosine, cosine], axis=1),
        jnp.concatenate([-sine_part, sine_part], axis=1),
    )


def attend_kernel(first, block, lows, starts, query, key, value, out, log_total):
    index = pl.program_id(1)
    begin = (first + index) * block
    queries = query[...]
    start = starts[...]
    place = begin + lax.broadcasted_iota(jnp.int32, (1, block), 1)

    def body(step, carry):
        peak, total, held = carry
        rows = pl.ds(pl.multiple_of(step * block, block), block)
        scores = lax.dot_general(
            key[rows, :], queries, (((1,), (1,)), ((), ())), preferred_element_type=WIDE
        )
        key_place = step * block + lax.broadcasted_iota(jnp.int32, (block, 1), 0)
        scores = jnp.where((key_place >= start) & (key_place <= place), scores, MASKED)
        top = jnp.maximum(peak, jnp.max(scores, axis=0, keepdims=True))
        weights = jnp.exp(scores - top)
        fade = jnp.exp(peak - top)
        total = total * fade + jnp.sum(weights, axis=0, keepdims=True)
        held = held * fade + lax.dot_general(
            value[rows, :], weights.astype(LOW), (((0,), (0,)), ((), ())), preferred_element_type=WIDE
        )
        return (top, total, held)

    row = jnp.full((1, block), MASKED, WIDE)
    carry = (row, jnp.zeros((1, block), WIDE), jnp.zeros((HEAD_DIM, block), WIDE))
    peak, total, held = lax.fori_loop(lows[first + index], first + index + 1, body, carry)
    out[...] = (held / total).T.astype(LOW)
    log_total[0] = peak + jnp.log(total)


def attend(lows, starts, query, key, value, first, count, block):
    length, local = query.shape
    heads = local // HEAD_DIM
    rows = count * block
    own = pl.BlockSpec((block, HEAD_DIM), lambda h, i, _: (first + i, h))
    all_keys = pl.BlockSpec((length, HEAD_DIM), lambda h, i, _: (0, h))
    made = pl.BlockSpec((block, HEAD_DIM), lambda h, i, _: (i, h))
    return pl.pallas_call(
        functools.partial(attend_kernel, first, block),
        grid_spec=pltpu.PrefetchScalarGridSpec(
            num_scalar_prefetch=1,
            grid=(heads, count),
            in_specs=[pl.BlockSpec((1, block), lambda h, i, _: (0, first + i)), own, all_keys, all_keys],
            out_specs=[made, pl.BlockSpec((1, 1, block), lambda h, i, _: (h, 0, i))],
        ),
        out_shape=[
            jax.ShapeDtypeStruct((rows, local), LOW),
            jax.ShapeDtypeStruct((heads, 1, rows), WIDE),
        ],
        compiler_params=params(),
        cost_estimate=pl.CostEstimate(
            flops=8 * rows * 1024 * local, bytes_accessed=12 * length * local, transcendentals=0
        ),
    )(lows, starts, query, key, value)


def attend_back_kernel(
    block, lows, starts, query, key, value, log_total, out, grads, dquery, dkey, dvalue
):
    index = pl.program_id(1)
    begin = index * block
    queries, out_grads = query[...], grads[...]
    start = starts[...]
    place = begin + lax.broadcasted_iota(jnp.int32, (1, block), 1)
    lse = log_total[0]
    products = out_grads.astype(WIDE) * out[...].astype(WIDE)
    less = jnp.sum(products.T, axis=0, keepdims=True)

    @pl.when(index == 0)
    def _():
        dkey[...] = jnp.zeros_like(dkey)
        dvalue[...] = jnp.zeros_like(dvalue)

    def body(step, held):
        rows = pl.ds(pl.multiple_of(step * block, block), block)
        keys_here = key[rows, :]
        across = (((1,), (1,)), ((), ()))
        scores = lax.dot_general(keys_here, queries, across, preferred_element_type=WIDE)
        key_place = step * block + lax.broadcasted_iota(jnp.int32, (block, 1), 0)
        allowed = (key_place >= start) & (key_place <= place)
        weights = jnp.exp(jnp.where(allowed, scores - lse, MASKED))
        back = lax.dot_general(value[rows, :], out_grads, across, preferred_element_type=WIDE)
        score_back = (weights * (back - less)).astype(LOW)
        dvalue[rows, :] += jnp.dot(weights.astype(LOW), out_grads, preferred_element_type=WIDE)
        dkey[rows, :] += jnp.dot(score_back, queries, preferred_element_type=WIDE)
        return held + lax.dot_general(
            keys_here, score_back, (((0,), (0,)), ((), ())), preferred_element_type=WIDE
        )

    held = lax.fori_loop(lows[index], index + 1, body, jnp.zeros((HEAD_DIM, block), WIDE))
    dquery[...] = held.T


def attend_back(lows, starts, query, key, value, log_total, out, grads, block):
    length, local = query.shape
    heads = local // HEAD_DIM
    own = pl.BlockSpec((block, HEAD_DIM), lambda h, i, _: (i, h))
    full = pl.BlockSpec((length, HEAD_DIM), lambda h, i, _: (0, h))
    line = pl.BlockSpec((1, 1, block), lambda h, i, _: (h, 0, i))
    shape = jax.ShapeDtypeStruct((length, local), WIDE)
    return pl.pallas_call(
        functools.partial(attend_back_kernel, block),
        grid_spec=pltpu.PrefetchScalarGridSpec(
            num_scalar_prefetch=1,
            grid=(heads, length // block),
            in_specs=[
                pl.BlockSpec((1, block), lambda h, i, _: (0, i)),
                own,
                full,
                full,
                line,
                own,
                own,
            ],
            out_specs=[own, full, full],
        ),
        out_shape=[shape, shape, shape],
        compiler_params=params(),
        cost_estimate=pl.CostEstimate(
            flops=20 * length * 1024 * local, bytes_accessed=20 * length * local, transcendentals=0
        ),
    )(lows, starts, query, key, value, log_total, out, grads)


def norm_back(cot_hat, raw, scale_rows, gain, total, width):
    return scale_rows * (cot_hat * gain) - raw * scale_rows**3 * (total[:, None] / width)


class Layout:
    def __init__(self, rows, cols):
        self.rows, self.cols = rows, cols
        self.half = cols // 2
        self.per = cols // rows

    def name(self, row, col):
        core, x = row & 1, row >> 1
        high, low = col // self.half, col % self.half
        return (x * 2 + high, core * self.half + low)

    def place(self, group, rank):
        x, high = group >> 1, group & 1
        core, low = rank // self.half, rank % self.half
        return (x * 2 + core) * self.cols + high * self.half + low

    def pairs(self, target):
        out = []
        for row in range(self.rows):
            for col in range(self.cols):
                out.append((row * self.cols + col, target(row, col)))
        return out

    def across_ranks(self, mask):
        def target(row, col):
            group, rank = self.name(row, col)
            return self.place(group, rank ^ mask)

        return self.pairs(target)

    def across_groups(self, mask):
        def target(row, col):
            group, rank = self.name(row, col)
            return self.place(group ^ mask, rank)

        return self.pairs(target)

    def exchange(self, flip):
        def target(row, col):
            core, x = row & 1, row >> 1
            high, low = col // self.half, col % self.half
            return (x * 2 + high) * self.cols + (core ^ flip) * self.half + low

        return self.pairs(target)

    def exchange_back(self, flip):
        return [(b, a) for a, b in self.exchange(flip)]


def send(values, pairs):
    return lax.ppermute(values, ("rows", "cols"), pairs)


class Chain:
    def __init__(self):
        self.last = None

    def send(self, values, pairs):
        if self.last is not None:
            values, self.last = lax.optimization_barrier((values, self.last))
        self.last = send(values, pairs)
        return self.last


def pick(values, places):
    if len(places) == 1:
        return values[places[0]][None]
    gap = places[1] - places[0]
    if places == list(range(places[0], places[-1] + 1, gap)):
        return values[places[0] : places[-1] + 1 : gap]
    return jnp.stack([values[p] for p in places])


def after(values, *others):
    return lax.optimization_barrier((values, *others))[0]


def params():
    return pltpu.CompilerParams(vmem_limit_bytes=VMEM)


def whole(shape):
    zeros = (0,) * len(shape)
    return pl.BlockSpec(shape, lambda *_: zeros, pipeline_mode=pl.Buffered(1))


def gather_pieces(ids, pieces, names, wide, per):
    rank, group = ids[0], ids[1]
    width = pieces[0].shape[-1]
    shift = per.bit_length() - 1
    for piece, numbers in zip(pieces, names, strict=True):
        for place, index in enumerate(numbers):
            block = jnp.bitwise_xor(rank, index)
            shard = jnp.bitwise_xor(lax.shift_right_logical(block, shift), group)
            inside = jnp.bitwise_and(block, per - 1)
            columns = pl.ds(pl.multiple_of(inside * width, width), width)
            wide[shard, :, columns] = piece[place]


def dot_rows(wide, shards, turned):
    dims = (((1,), (1,)), ((), ())) if turned else (((1,), (0,)), ((), ()))
    total = None
    for index, shard in enumerate(shards):
        part = lax.dot_general(wide[index], shard, dims, preferred_element_type=WIDE)
        total = part if total is None else total + part
    return total


def rows_kernel(names, count, shards, per, turned, epilogue, extra, merged, ids, *refs):
    pieces, refs = refs[: len(names)], refs[len(names) :]
    stacks, refs = refs[:shards], refs[shards:]
    extras, outs = refs[:extra], refs[extra + merged :]
    wide = outs[-1]
    gather_pieces(ids, pieces, names, wide, per)
    results = [dot_rows(wide, [stack[n] for stack in stacks], turned) for n in range(count)]
    epilogue(results, extras, outs[:-1])


def matmul_rows(ids, pieces, names, stacks, per, turned, epilogue, extras, out_types, into, block):
    rows, width = pieces[0].shape[1:]
    chunk, chunks, earlier = into
    shards = len(stacks)
    count = stacks[0].shape[0]
    block = min(block, rows)
    wide_width = per * width
    first = chunk * (rows // block)

    def tall(columns, merge=False):
        offset = first if merge else 0
        return pl.BlockSpec((block, columns), lambda i, _: (i + offset, 0))

    in_specs = [pl.BlockSpec((p.shape[0], block, width), lambda i, _: (0, i, 0)) for p in pieces]
    in_specs += [whole(stack.shape) for stack in stacks]
    in_specs += [tall(extra.shape[1]) for extra in extras]
    out_specs = [tall(columns, merge) for columns, _, merge in out_types]
    out_specs.append(pl.BlockSpec((shards, block, wide_width), lambda i, _: (0, i + first, 0)))
    out_shape = [
        jax.ShapeDtypeStruct((rows * chunks if merge else rows, columns), kind)
        for columns, kind, merge in out_types
    ]
    out_shape.append(jax.ShapeDtypeStruct((shards, rows * chunks, wide_width), LOW))
    merged = [i for i, kind in enumerate(out_types) if kind[2]] + [len(out_types)]
    handed = [] if earlier is None else [earlier[i] for i in merged]
    in_specs += [pl.BlockSpec(memory_space=pl.ANY) for _ in handed]
    operands = [ids, *pieces, *stacks, *extras]
    aliases = {len(operands) + n: i for n, i in enumerate(merged)} if handed else {}
    body = functools.partial(
        rows_kernel, names, count, shards, per, turned, epilogue, len(extras), len(handed)
    )
    size = sum(a.size * a.dtype.itemsize for a in operands)
    size += sum(columns * rows * jnp.dtype(kind).itemsize for columns, kind, _ in out_types)
    flops = 2 * rows * stacks[0].size * shards
    return pl.pallas_call(
        body,
        grid_spec=pltpu.PrefetchScalarGridSpec(
            num_scalar_prefetch=1,
            grid=(rows // block,),
            in_specs=in_specs,
            out_specs=out_specs,
        ),
        out_shape=out_shape,
        input_output_aliases=aliases,
        compiler_params=params(),
        cost_estimate=pl.CostEstimate(flops=flops, bytes_accessed=size, transcendentals=0),
    )(*operands, *handed)


def columns_kernel(count, shards, per, turned, ids, *refs):
    lefts, stacks = refs[:count], refs[count : count + shards]
    keep, give, held = refs[count + shards :]
    rank, group = ids[0], ids[1]
    half, _, width = keep.shape
    shift = per.bit_length() - 1
    dims = (((1,), (1,)), ((), ())) if turned else (((1,), (0,)), ((), ()))
    for index, stack in enumerate(stacks):
        total = None
        for number, left in enumerate(lefts):
            part = lax.dot_general(left[...], stack[number], dims, preferred_element_type=WIDE)
            total = part if total is None else total + part
        total = total.astype(LOW)
        base = lax.shift_left(jnp.bitwise_xor(group, index), shift)
        for inside in range(per):
            piece = jnp.bitwise_xor(base + inside, rank)
            held[piece] = total[:, inside * width : (inside + 1) * width]
    keep[...] = held[:half]
    give[...] = held[half:]


def matmul_columns(ids, lefts, offset, rows, stacks, per, ranks, turned, block):
    block = min(block, rows)
    shards = len(stacks)
    width = stacks[0].shape[1 if turned else 2] // per
    first = offset // block
    in_specs = [
        pl.BlockSpec((block, left.shape[1]), lambda i, _: (i + first, 0)) for left in lefts
    ]
    in_specs += [whole(stack.shape) for stack in stacks]
    part = pl.BlockSpec((ranks // 2, block, width), lambda i, _: (0, i, 0))
    shape = jax.ShapeDtypeStruct((ranks // 2, rows, width), LOW)
    size = sum(rows * left.shape[1] * 2 for left in lefts) + 4 * shape.size
    size += sum(stack.size * 2 for stack in stacks)
    flops = 2 * rows * stacks[0].size * shards
    return pl.pallas_call(
        functools.partial(columns_kernel, len(lefts), shards, per, turned),
        grid_spec=pltpu.PrefetchScalarGridSpec(
            num_scalar_prefetch=1,
            grid=(rows // block,),
            in_specs=in_specs,
            out_specs=[part, part],
            scratch_shapes=[pltpu.VMEM((ranks, block, width), LOW)],
        ),
        out_shape=[shape, shape],
        compiler_params=params(),
        cost_estimate=pl.CostEstimate(flops=flops, bytes_accessed=size, transcendentals=0),
    )(ids, *lefts, *stacks)


def tall_kernel(counts, half, wide_left, wide, *refs):
    talls, (keep, give) = refs[: sum(counts)], refs[sum(counts) :]
    results = []
    for count in counts:
        total, offset = None, 0
        for tall in talls[:count]:
            rows = tall.shape[0]
            sides = (wide[0, offset : offset + rows, :], tall[...])
            left, right = sides if wide_left else sides[::-1]
            dims = (((0,), (0,)), ((), ()))
            part = lax.dot_general(left, right, dims, preferred_element_type=WIDE)
            total = part if total is None else total + part
            offset += rows
        talls = talls[count:]
        results.append(total.astype(LOW))

    @pl.when(pl.program_id(0) < half)
    def _():
        for number, result in enumerate(results):
            give[0, number] = result

    @pl.when(pl.program_id(0) >= half)
    def _():
        for number, result in enumerate(results):
            keep[0, number] = result


def matmul_tall(wide, groups, wide_left, block):
    shards, length, features = wide.shape
    columns = groups[0][0].shape[1]
    half = shards // 2
    count = len(groups)
    talls = [tall for group in groups for tall in group]

    def order(i):
        return lax.rem(i + half, shards)

    if wide_left:
        block = min(block, features)
        steps = features // block
        in_specs = [pl.BlockSpec((1, length, block), lambda i, j: (order(i), 0, j))]
        in_specs += [whole(tall.shape) for tall in talls]
        tile = (1, count, block, columns)
        full = (half, count, features, columns)
    else:
        block = min(block, columns)
        steps = columns // block
        in_specs = [pl.BlockSpec((1, length, features), lambda i, j: (order(i), 0, 0))]
        in_specs += [pl.BlockSpec((tall.shape[0], block), lambda i, j: (0, j)) for tall in talls]
        tile = (1, count, block, features)
        full = (half, count, columns, features)

    def give_place(i, j):
        ahead = i < half
        return (jnp.where(ahead, i, half - 1), 0, jnp.where(ahead, j, steps - 1), 0)

    def keep_place(i, j):
        ahead = i < half
        return (jnp.where(ahead, 0, i - half), 0, jnp.where(ahead, 0, j), 0)

    shape = jax.ShapeDtypeStruct(full, LOW)
    size = wide.size * 2 + sum(tall.size * 2 for tall in talls) + 4 * shape.size
    return pl.pallas_call(
        functools.partial(tall_kernel, [len(g) for g in groups], half, wide_left),
        grid=(shards, steps),
        in_specs=in_specs,
        out_specs=[pl.BlockSpec(tile, keep_place), pl.BlockSpec(tile, give_place)],
        out_shape=[shape, shape],
        compiler_params=params(),
        cost_estimate=pl.CostEstimate(
            flops=2 * wide.size * columns * count, bytes_accessed=size, transcendentals=0
        ),
    )(wide, *talls)


def prepare_kernel(scale, query, key, scales, gains, cosine, sine_part, query_low, key_low):
    heads = query.shape[1] // HEAD_DIM
    columns = scales[...].T
    for source, target, number, factor in ((query, query_low, 0, scale), (key, key_low, 1, 1.0)):
        normed = source[...] * columns[:, number : number + 1] * gains[number : number + 1, :]
        for head in range(heads):
            part = normed[:, head * HEAD_DIM : (head + 1) * HEAD_DIM]
            spun = part * cosine[...] + pltpu.roll(part, HEAD_DIM // 2, 1) * sine_part[...]
            target[:, head * HEAD_DIM : (head + 1) * HEAD_DIM] = (spun * factor).astype(LOW)


def prepare(query, key, scales, gains, cosine, sine_part, scale, block):
    length, local = query.shape
    tall = pl.BlockSpec((block, local), lambda i: (i, 0))
    table = pl.BlockSpec((block, HEAD_DIM), lambda i: (i, 0))
    shape = jax.ShapeDtypeStruct((length, local), LOW)
    return pl.pallas_call(
        functools.partial(prepare_kernel, scale),
        grid=(length // block,),
        in_specs=[
            tall,
            tall,
            pl.BlockSpec((8, block), lambda i: (0, i)),
            whole(gains.shape),
            table,
            table,
        ],
        out_specs=[tall, tall],
        out_shape=[shape, shape],
        compiler_params=params(),
        cost_estimate=pl.CostEstimate(
            flops=20 * query.size, bytes_accessed=12 * query.size, transcendentals=0
        ),
    )(query, key, scales, gains, cosine, sine_part)


def unturn_kernel(
    scale, query, key, query_grad, key_grad, scales, gains, cosine, sine_part, *outs
):
    query_hat, key_hat, sums, gain_sums = outs
    heads = query.shape[1] // HEAD_DIM
    columns = scales[...].T
    lines, gain_rows = [], []
    for raw, grad, target, number, factor in (
        (query, query_grad, query_hat, 0, scale),
        (key, key_grad, key_hat, 1, 1.0),
    ):
        for head in range(heads):
            part = slice(head * HEAD_DIM, (head + 1) * HEAD_DIM)
            back = grad[:, part] * factor
            target[:, part] = back * cosine[...] - pltpu.roll(back, HEAD_DIM // 2, 1) * sine_part[...]
        product = target[...] * raw[...]
        gain_rows.append(
            jnp.sum(product * columns[:, number : number + 1], axis=0, keepdims=True)
        )
        weighted = product * gains[number : number + 1, :]
        lines.append(jnp.sum(weighted, axis=1, keepdims=True))
    spread = jnp.concatenate(lines + [jnp.zeros((query.shape[0], 6), WIDE)], axis=1)
    sums[...] = spread.T

    @pl.when(pl.program_id(0) == 0)
    def _():
        gain_sums[...] = jnp.zeros_like(gain_sums)

    for number, line in enumerate(gain_rows):
        gain_sums[number : number + 1, :] += line


def unturn(query, key, query_grad, key_grad, scales, gains, cosine, sine_part, scale, block):
    length, local = query.shape
    tall = pl.BlockSpec((block, local), lambda i: (i, 0))
    table = pl.BlockSpec((block, HEAD_DIM), lambda i: (i, 0))
    line = pl.BlockSpec((8, block), lambda i: (0, i))
    shape = jax.ShapeDtypeStruct((length, local), WIDE)
    return pl.pallas_call(
        functools.partial(unturn_kernel, scale),
        grid=(length // block,),
        in_specs=[tall, tall, tall, tall, line, whole(gains.shape), table, table],
        out_specs=[tall, tall, line, pl.BlockSpec((8, local), lambda i: (0, 0))],
        out_shape=[
            shape,
            shape,
            jax.ShapeDtypeStruct((8, length), WIDE),
            jax.ShapeDtypeStruct((8, local), WIDE),
        ],
        compiler_params=params(),
        cost_estimate=pl.CostEstimate(
            flops=20 * query.size, bytes_accessed=24 * query.size, transcendentals=0
        ),
    )(query, key, query_grad, key_grad, scales, gains, cosine, sine_part)


def query_key_value(results, _, outs):
    query, key, value = results
    outs[0][...] = query
    outs[1][...] = key
    outs[2][...] = value.astype(LOW)


def gated(results, _, outs):
    gate, upward = results
    outs[0][...] = (gate * jax.nn.sigmoid(gate) * upward).astype(LOW)
    outs[1][...] = gate.astype(LOW)
    outs[2][...] = upward.astype(LOW)


def gated_back(results, extras, outs):
    mixed_back = results[0]
    gate = extras[0][...].astype(WIDE)
    upward = extras[1][...].astype(WIDE)
    gate_sig = jax.nn.sigmoid(gate)
    outs[0][...] = (mixed_back * upward * gate_sig * (1.0 + gate * (1.0 - gate_sig))).astype(LOW)
    outs[1][...] = (mixed_back * gate * gate_sig).astype(LOW)


def just_low(results, _, outs):
    outs[0][...] = results[0].astype(LOW)


def per_device(
    layout,
    tokens,
    segment_ids,
    w_query,
    w_key,
    w_value,
    w_out,
    w_gate,
    w_up,
    w_down,
    q_gain,
    k_gain,
    attn_gain,
    ffn_gain,
    out_grad,
):
    seq_len = segment_ids.shape[1]
    rows, local = tokens.shape
    ranks, groups, per = layout.cols, layout.rows, layout.per
    model = local * ranks
    hidden_units = w_gate.shape[1]
    scale = HEAD_DIM ** (-0.5)
    chunks = CHUNKS
    step = rows // chunks
    cuts = [(c * step, (c + 1) * step) for c in range(chunks)]
    row, col = lax.axis_index("rows"), lax.axis_index("cols")
    group = (row // 2) * 2 + col // layout.half
    rank = (row % 2) * layout.half + col % layout.half
    ids = jnp.stack([rank, group]).astype(jnp.int32)
    rank_bits = [1 << i for i in range(ranks.bit_length() - 1)]
    group_bits = [1 << i for i in range(1, groups.bit_length() - 1)]
    cores = rank_bits[-1]

    def links(index):
        return rank_bits[:-1] if index % 2 else rank_bits[:-1][::-1]

    def piece_names(index):
        found = [(0,)]
        for mask in [*links(index), cores]:
            found.append(tuple(j ^ mask for names in found for j in names))
        return found

    far, side = Chain(), Chain()

    def spread(piece, index):
        pieces = [piece[None]]
        for mask in [*links(index), cores]:
            whole_part = pieces[0] if len(pieces) == 1 else jnp.concatenate(pieces)
            pieces.append(send(whole_part, layout.across_ranks(mask)))
        return pieces

    def totals(stacked):
        for mask in rank_bits:
            stacked = stacked + send(stacked, layout.across_ranks(mask))
        return stacked

    def reduce(keep, give, index):
        arrived = send(give, layout.across_ranks(cores))
        names = list(range(cores))
        for mask in links(index + 1):
            total = (keep.astype(WIDE) + arrived.astype(WIDE)).astype(LOW)
            stay = [n for n, name in enumerate(names) if not name & mask]
            leave = [names.index(names[n] ^ mask) for n in stay]
            keep, give = pick(total, stay), pick(total, leave)
            names = [names[n] for n in stay]
            arrived = send(give, layout.across_ranks(mask))
        return keep[0].astype(WIDE) + arrived[0].astype(WIDE)

    def whole_weight(stack):
        found = [far.send(stack, layout.exchange(0)), far.send(stack, layout.exchange(1))]
        for mask in group_bits:
            found += [side.send(v, layout.across_groups(mask)) for v in found]
        return found

    def owners_sum(keep, give):
        for mask in group_bits[::-1]:
            arrived = side.send(give, layout.across_groups(mask))
            total = (keep.astype(WIDE) + arrived.astype(WIDE)).astype(LOW)
            size = total.shape[0] // 2
            keep, give = total[:size], total[size:]
        mine = far.send(keep[0], layout.exchange_back(0))
        other = far.send(give[0], layout.exchange_back(1))
        count = mine.shape[0]
        return [mine[n].astype(WIDE) + other[n].astype(WIDE) for n in range(count)]

    tokens = send(tokens, layout.exchange(0))
    full_qkv = whole_weight(jnp.stack([w_query, w_key, w_value]))
    gains = send(jnp.stack([q_gain, k_gain, attn_gain, ffn_gain]), layout.exchange(0))
    attn_gain, ffn_gain = gains[2], gains[3]
    segment_ids = send(segment_ids, layout.exchange(0))
    full_out = whole_weight(w_out[None])
    full_gated = whole_weight(jnp.stack([w_gate, w_up]))
    full_down = whole_weight(w_down[None])
    out_grad = far.send(out_grad, layout.exchange(0))
    cosine, sine_part = rotation(seq_len, HEAD_DIM)

    made = None
    for index, (low, high) in enumerate(cuts):
        made = matmul_rows(
            ids,
            spread(tokens[low:high], index),
            piece_names(index),
            full_qkv,
            per,
            False,
            query_key_value,
            [],
            [(local, WIDE, True), (local, WIDE, True), (local, LOW, True)],
            (index, chunks, made),
            256,
        )
    query_raw, key_raw, value_low, token_wide = made
    qk_stats = totals(
        jnp.stack([jnp.sum(query_raw * query_raw, axis=1), jnp.sum(key_raw * key_raw, axis=1)])
    )
    scales = jnp.pad(lax.rsqrt(qk_stats / model + EPS), ((0, 6), (0, 0)))
    block = min(512, seq_len)
    query_low, key_low = prepare(
        query_raw, key_raw, scales, gains, cosine, sine_part, scale, block
    )
    names = jnp.arange(DOCUMENTS, dtype=jnp.int32)[:, None]
    before = jnp.sum((segment_ids < names).astype(jnp.int32), axis=1, keepdims=True)
    starts = jnp.sum(jnp.where(segment_ids == names, before, 0), axis=0, keepdims=True)
    lows = starts[0, ::block] // block
    per_chunk = step // block
    columns = functools.partial(matmul_columns, ids, per=per, ranks=ranks, block=256)
    attn_parts, log_totals, out_sums = [], [], []
    for index in range(chunks):
        if index:
            query_low = after(query_low, out_sums[-1])
        out, log_total = attend(
            lows, starts, query_low, key_low, value_low, index * per_chunk, per_chunk, block
        )
        out_sums.append(columns([out], 0, step, full_out, turned=False))
        attn_parts.append(out)
        log_totals.append(log_total)

    def mean_scale(stats):
        return lax.rsqrt(stats / model + EPS)[:, None]

    hidden_made, ffn_made, attn_made = None, None, None
    mixes, gate_backs, up_backs, hidden_cots, layer_outs = [], [], [], [], []
    gain_attn, gain_ffn = 0.0, 0.0
    for index, (low, high) in enumerate(cuts):
        attn_sum = reduce(*out_sums[index], index)
        attn_scale = mean_scale(totals(jnp.sum(attn_sum * attn_sum, axis=1)[None])[0])
        hidden = tokens[low:high].astype(WIDE) + attn_sum * attn_scale * attn_gain
        pieces = spread(hidden.astype(LOW), index)
        if index:
            pieces = after(pieces, forward_last)
        hidden_made = matmul_rows(
            ids,
            pieces,
            piece_names(index),
            full_gated,
            per,
            False,
            gated,
            [],
            [(hidden_units, LOW, False)] * 3,
            (index, chunks, hidden_made),
            256,
        )
        mixed, gate, upward = hidden_made[:3]
        forward_last = columns([mixed], 0, step, full_down, turned=False)
        ffn_sum = reduce(*forward_last, index)
        out_cot = out_grad[low:high].astype(WIDE)
        stats = totals(
            jnp.stack(
                [
                    jnp.sum(ffn_sum * ffn_sum, axis=1),
                    jnp.sum(out_cot * ffn_gain * ffn_sum, axis=1),
                ]
            )
        )
        ffn_scale = mean_scale(stats[0])
        layer_outs.append((hidden + ffn_sum * ffn_scale * ffn_gain).astype(LOW))
        gain_ffn = gain_ffn + jnp.sum(out_cot * ffn_sum * ffn_scale, axis=0)
        ffn_back = norm_back(out_cot, ffn_sum, ffn_scale, ffn_gain, stats[1], model).astype(LOW)
        pieces = spread(ffn_back, index)
        if index:
            pieces = after(pieces, backward_last)
        ffn_made = matmul_rows(
            ids,
            pieces,
            piece_names(index),
            full_down,
            per,
            True,
            gated_back,
            [gate, upward],
            [(hidden_units, LOW, False)] * 2,
            (index, chunks, ffn_made),
            256,
        )
        gate_back, up_back = ffn_made[:2]
        backward_last = columns([gate_back, up_back], 0, step, full_gated, turned=True)
        hidden_cot = out_cot + reduce(*backward_last, index)
        attn_total = totals(jnp.sum(hidden_cot * attn_gain * attn_sum, axis=1)[None])[0]
        gain_attn = gain_attn + jnp.sum(hidden_cot * attn_sum * attn_scale, axis=0)
        attn_back = norm_back(
            hidden_cot, attn_sum, attn_scale, attn_gain, attn_total, model
        ).astype(LOW)
        attn_made = matmul_rows(
            ids,
            spread(attn_back, index),
            piece_names(index),
            full_out,
            per,
            True,
            just_low,
            [],
            [(local, LOW, True)],
            (index, chunks, attn_made),
            256,
        )
        mixes.append(mixed)
        gate_backs.append(gate_back)
        up_backs.append(up_back)
        hidden_cots.append(hidden_cot)

    layer_out = far.send(jnp.concatenate(layer_outs), layout.exchange_back(0))
    grad_down = owners_sum(*matmul_tall(ffn_made[-1], [mixes], False, 512))[0]
    grad_gate, grad_up = owners_sum(
        *matmul_tall(hidden_made[-1], [gate_backs, up_backs], True, 256)
    )
    out_back, attn_wide = attn_made
    grad_out = owners_sum(*matmul_tall(attn_wide, [attn_parts], False, 256))[0]

    query_grad, key_grad, value_grad = attend_back(
        lows,
        starts,
        query_low,
        key_low,
        value_low,
        jnp.concatenate(log_totals, axis=2),
        jnp.concatenate(attn_parts),
        out_back,
        block,
    )
    value_back = value_grad.astype(LOW)
    query_hat, key_hat, sums, gain_sums = unturn(
        query_raw,
        key_raw,
        query_grad,
        key_grad,
        scales,
        gains,
        cosine,
        sine_part,
        scale,
        block,
    )
    qk_totals = totals(sums[:2])
    query_back = norm_back(
        query_hat, query_raw, scales[0][:, None], gains[0], qk_totals[0], model
    ).astype(LOW)
    key_back = norm_back(
        key_hat, key_raw, scales[1][:, None], gains[1], qk_totals[1], model
    ).astype(LOW)

    input_grads = []
    for index, (low, high) in enumerate(cuts):
        total = columns([query_back, key_back, value_back], low, step, full_qkv, turned=True)
        total = reduce(*total, index)
        total = (hidden_cots[index] + total).astype(LOW)
        input_grads.append(send(total, layout.exchange_back(0)))
    input_grad = jnp.concatenate(input_grads)
    grad_query, grad_key, grad_value = owners_sum(
        *matmul_tall(token_wide, [[query_back], [key_back], [value_back]], True, 512)
    )

    gains = jnp.concatenate([gain_sums[:2], gain_attn[None], gain_ffn[None]])
    for mask in [1, *group_bits]:
        gains = gains + send(gains, layout.across_groups(mask))
    gains = send(gains, layout.exchange_back(0))
    return (
        layer_out,
        input_grad,
        grad_query,
        grad_key,
        grad_value,
        grad_out,
        grad_gate,
        grad_up,
        grad_down,
        gains[0],
        gains[1],
        gains[2],
        gains[3],
    )


def solution(mesh):
    layout = Layout(mesh.shape["rows"], mesh.shape["cols"])
    both, turned, lone = P("rows", "cols"), P("cols", "rows"), P("cols")
    in_specs = (both, P("rows", None), both, both, both, turned, both, both, turned)
    in_specs += (lone, lone, lone, lone, both)
    out_specs = (both, both, both, both, both, turned, both, both, turned)
    out_specs += (lone, lone, lone, lone)
    return jax.shard_map(
        functools.partial(per_device, layout),
        mesh=mesh,
        in_specs=in_specs,
        out_specs=out_specs,
        check_vma=False,
    )
```

```python
import functools

import jax
import jax.numpy as jnp
from jax import lax
from jax.experimental import pallas as pl
from jax.experimental.pallas import tpu as pltpu
from jax.sharding import PartitionSpec as P

HEAD_DIM = 128
EPS = 1e-06
THETA = 500000.0
MASKED = -1e30
LOW = jnp.bfloat16
WIDE = jnp.float32
CHUNKS = 4
DOCUMENTS = 8
VMEM = 52 * 2**20


def rotation(length, width):
    halfway = width // 2
    rates = THETA ** (-2.0 * jnp.arange(halfway, dtype=WIDE) / width)
    angles = jnp.arange(length, dtype=WIDE)[:, None] * rates[None, :]
    cosine, sine_part = jnp.cos(angles), jnp.sin(angles)
    return (
        jnp.concatenate([cosine, cosine], axis=1),
        jnp.concatenate([-sine_part, sine_part], axis=1),
    )


def attend_kernel(first, block, lows, starts, query, key, value, out, log_total):
    index = pl.program_id(1)
    begin = (first + index) * block
    queries = query[...]
    start = starts[...]
    place = begin + lax.broadcasted_iota(jnp.int32, (1, block), 1)

    def body(step, carry):
        peak, total, held = carry
        rows = pl.ds(pl.multiple_of(step * block, block), block)
        scores = lax.dot_general(
            key[rows, :], queries, (((1,), (1,)), ((), ())), preferred_element_type=WIDE
        )
        key_place = step * block + lax.broadcasted_iota(jnp.int32, (block, 1), 0)
        scores = jnp.where((key_place >= start) & (key_place <= place), scores, MASKED)
        top = jnp.maximum(peak, jnp.max(scores, axis=0, keepdims=True))
        weights = jnp.exp(scores - top)
        fade = jnp.exp(peak - top)
        total = total * fade + jnp.sum(weights, axis=0, keepdims=True)
        held = held * fade + lax.dot_general(
            value[rows, :], weights.astype(LOW), (((0,), (0,)), ((), ())), preferred_element_type=WIDE
        )
        return (top, total, held)

    row = jnp.full((1, block), MASKED, WIDE)
    carry = (row, jnp.zeros((1, block), WIDE), jnp.zeros((HEAD_DIM, block), WIDE))
    peak, total, held = lax.fori_loop(lows[first + index], first + index + 1, body, carry)
    out[...] = (held / total).T.astype(LOW)
    log_total[0] = peak + jnp.log(total)


def attend(lows, starts, query, key, value, first, count, block):
    length, local = query.shape
    heads = local // HEAD_DIM
    rows = count * block
    own = pl.BlockSpec((block, HEAD_DIM), lambda h, i, _: (first + i, h))
    all_keys = pl.BlockSpec((length, HEAD_DIM), lambda h, i, _: (0, h))
    made = pl.BlockSpec((block, HEAD_DIM), lambda h, i, _: (i, h))
    return pl.pallas_call(
        functools.partial(attend_kernel, first, block),
        grid_spec=pltpu.PrefetchScalarGridSpec(
            num_scalar_prefetch=1,
            grid=(heads, count),
            in_specs=[pl.BlockSpec((1, block), lambda h, i, _: (0, first + i)), own, all_keys, all_keys],
            out_specs=[made, pl.BlockSpec((1, 1, block), lambda h, i, _: (h, 0, i))],
        ),
        out_shape=[
            jax.ShapeDtypeStruct((rows, local), LOW),
            jax.ShapeDtypeStruct((heads, 1, rows), WIDE),
        ],
        compiler_params=params(),
        cost_estimate=pl.CostEstimate(
            flops=8 * rows * 1024 * local, bytes_accessed=12 * length * local, transcendentals=0
        ),
    )(lows, starts, query, key, value)


def attend_back_kernel(
    block, lows, starts, query, key, value, log_total, out, grads, dquery, dkey, dvalue
):
    index = pl.program_id(1)
    begin = index * block
    queries, out_grads = query[...], grads[...]
    start = starts[...]
    place = begin + lax.broadcasted_iota(jnp.int32, (1, block), 1)
    lse = log_total[0]
    products = out_grads.astype(WIDE) * out[...].astype(WIDE)
    less = jnp.sum(products.T, axis=0, keepdims=True)

    @pl.when(index == 0)
    def _():
        dkey[...] = jnp.zeros_like(dkey)
        dvalue[...] = jnp.zeros_like(dvalue)

    def body(step, held):
        rows = pl.ds(pl.multiple_of(step * block, block), block)
        keys_here = key[rows, :]
        across = (((1,), (1,)), ((), ()))
        scores = lax.dot_general(keys_here, queries, across, preferred_element_type=WIDE)
        key_place = step * block + lax.broadcasted_iota(jnp.int32, (block, 1), 0)
        allowed = (key_place >= start) & (key_place <= place)
        weights = jnp.exp(jnp.where(allowed, scores - lse, MASKED))
        back = lax.dot_general(value[rows, :], out_grads, across, preferred_element_type=WIDE)
        score_back = (weights * (back - less)).astype(LOW)
        dvalue[rows, :] += jnp.dot(weights.astype(LOW), out_grads, preferred_element_type=WIDE)
        dkey[rows, :] += jnp.dot(score_back, queries, preferred_element_type=WIDE)
        return held + lax.dot_general(
            keys_here, score_back, (((0,), (0,)), ((), ())), preferred_element_type=WIDE
        )

    held = lax.fori_loop(lows[index], index + 1, body, jnp.zeros((HEAD_DIM, block), WIDE))
    dquery[...] = held.T


def attend_back(lows, starts, query, key, value, log_total, out, grads, block):
    length, local = query.shape
    heads = local // HEAD_DIM
    own = pl.BlockSpec((block, HEAD_DIM), lambda h, i, _: (i, h))
    full = pl.BlockSpec((length, HEAD_DIM), lambda h, i, _: (0, h))
    line = pl.BlockSpec((1, 1, block), lambda h, i, _: (h, 0, i))
    shape = jax.ShapeDtypeStruct((length, local), WIDE)
    return pl.pallas_call(
        functools.partial(attend_back_kernel, block),
        grid_spec=pltpu.PrefetchScalarGridSpec(
            num_scalar_prefetch=1,
            grid=(heads, length // block),
            in_specs=[
                pl.BlockSpec((1, block), lambda h, i, _: (0, i)),
                own,
                full,
                full,
                line,
                own,
                own,
            ],
            out_specs=[own, full, full],
        ),
        out_shape=[shape, shape, shape],
        compiler_params=params(),
        cost_estimate=pl.CostEstimate(
            flops=20 * length * 1024 * local, bytes_accessed=20 * length * local, transcendentals=0
        ),
    )(lows, starts, query, key, value, log_total, out, grads)


def norm_back(cot_hat, raw, scale_rows, gain, total, width):
    return scale_rows * (cot_hat * gain) - raw * scale_rows**3 * (total[:, None] / width)


class Layout:
    def __init__(self, rows, cols):
        self.rows, self.cols = rows, cols
        self.half = cols // 2
        self.per = cols // rows

    def name(self, row, col):
        core, x = row & 1, row >> 1
        high, low = col // self.half, col % self.half
        return (x * 2 + high, core * self.half + low)

    def place(self, group, rank):
        x, high = group >> 1, group & 1
        core, low = rank // self.half, rank % self.half
        return (x * 2 + core) * self.cols + high * self.half + low

    def pairs(self, target):
        out = []
        for row in range(self.rows):
            for col in range(self.cols):
                out.append((row * self.cols + col, target(row, col)))
        return out

    def across_ranks(self, mask):
        def target(row, col):
            group, rank = self.name(row, col)
            return self.place(group, rank ^ mask)

        return self.pairs(target)

    def across_groups(self, mask):
        def target(row, col):
            group, rank = self.name(row, col)
            return self.place(group ^ mask, rank)

        return self.pairs(target)

    def exchange(self, flip):
        def target(row, col):
            core, x = row & 1, row >> 1
            high, low = col // self.half, col % self.half
            return (x * 2 + high) * self.cols + (core ^ flip) * self.half + low

        return self.pairs(target)

    def exchange_back(self, flip):
        return [(b, a) for a, b in self.exchange(flip)]


def send(values, pairs):
    return lax.ppermute(values, ("rows", "cols"), pairs)


class Chain:
    def __init__(self):
        self.last = None

    def send(self, values, pairs):
        if self.last is not None:
            values, self.last = lax.optimization_barrier((values, self.last))
        self.last = send(values, pairs)
        return self.last


def pick(values, places):
    if len(places) == 1:
        return values[places[0]][None]
    gap = places[1] - places[0]
    if places == list(range(places[0], places[-1] + 1, gap)):
        return values[places[0] : places[-1] + 1 : gap]
    return jnp.stack([values[p] for p in places])


def after(values, *others):
    return lax.optimization_barrier((values, *others))[0]


def params():
    return pltpu.CompilerParams(vmem_limit_bytes=VMEM)


def whole(shape):
    zeros = (0,) * len(shape)
    return pl.BlockSpec(shape, lambda *_: zeros, pipeline_mode=pl.Buffered(1))


def gather_pieces(ids, pieces, names, wide, per):
    rank, group = ids[0], ids[1]
    width = pieces[0].shape[-1]
    shift = per.bit_length() - 1
    for piece, numbers in zip(pieces, names, strict=True):
        for place, index in enumerate(numbers):
            block = jnp.bitwise_xor(rank, index)
            shard = jnp.bitwise_xor(lax.shift_right_logical(block, shift), group)
            inside = jnp.bitwise_and(block, per - 1)
            columns = pl.ds(pl.multiple_of(inside * width, width), width)
            wide[shard, :, columns] = piece[place]


def dot_rows(wide, shards, turned):
    dims = (((1,), (1,)), ((), ())) if turned else (((1,), (0,)), ((), ()))
    total = None
    for index, shard in enumerate(shards):
        part = lax.dot_general(wide[index], shard, dims, preferred_element_type=WIDE)
        total = part if total is None else total + part
    return total


def rows_kernel(names, count, shards, per, turned, epilogue, extra, merged, ids, *refs):
    pieces, refs = refs[: len(names)], refs[len(names) :]
    stacks, refs = refs[:shards], refs[shards:]
    extras, outs = refs[:extra], refs[extra + merged :]
    wide = outs[-1]
    gather_pieces(ids, pieces, names, wide, per)
    results = [dot_rows(wide, [stack[n] for stack in stacks], turned) for n in range(count)]
    epilogue(results, extras, outs[:-1])


def matmul_rows(ids, pieces, names, stacks, per, turned, epilogue, extras, out_types, into, block):
    rows, width = pieces[0].shape[1:]
    chunk, chunks, earlier = into
    shards = len(stacks)
    count = stacks[0].shape[0]
    block = min(block, rows)
    wide_width = per * width
    first = chunk * (rows // block)

    def tall(columns, merge=False):
        offset = first if merge else 0
        return pl.BlockSpec((block, columns), lambda i, _: (i + offset, 0))

    in_specs = [pl.BlockSpec((p.shape[0], block, width), lambda i, _: (0, i, 0)) for p in pieces]
    in_specs += [whole(stack.shape) for stack in stacks]
    in_specs += [tall(extra.shape[1]) for extra in extras]
    out_specs = [tall(columns, merge) for columns, _, merge in out_types]
    out_specs.append(pl.BlockSpec((shards, block, wide_width), lambda i, _: (0, i + first, 0)))
    out_shape = [
        jax.ShapeDtypeStruct((rows * chunks if merge else rows, columns), kind)
        for columns, kind, merge in out_types
    ]
    out_shape.append(jax.ShapeDtypeStruct((shards, rows * chunks, wide_width), LOW))
    merged = [i for i, kind in enumerate(out_types) if kind[2]] + [len(out_types)]
    handed = [] if earlier is None else [earlier[i] for i in merged]
    in_specs += [pl.BlockSpec(memory_space=pl.ANY) for _ in handed]
    operands = [ids, *pieces, *stacks, *extras]
    aliases = {len(operands) + n: i for n, i in enumerate(merged)} if handed else {}
    body = functools.partial(
        rows_kernel, names, count, shards, per, turned, epilogue, len(extras), len(handed)
    )
    size = sum(a.size * a.dtype.itemsize for a in operands)
    size += sum(columns * rows * jnp.dtype(kind).itemsize for columns, kind, _ in out_types)
    flops = 2 * rows * stacks[0].size * shards
    return pl.pallas_call(
        body,
        grid_spec=pltpu.PrefetchScalarGridSpec(
            num_scalar_prefetch=1,
            grid=(rows // block,),
            in_specs=in_specs,
            out_specs=out_specs,
        ),
        out_shape=out_shape,
        input_output_aliases=aliases,
        compiler_params=params(),
        cost_estimate=pl.CostEstimate(flops=flops, bytes_accessed=size, transcendentals=0),
    )(*operands, *handed)


def columns_kernel(count, shards, per, turned, ids, *refs):
    lefts, stacks = refs[:count], refs[count : count + shards]
    keep, give, held = refs[count + shards :]
    rank, group = ids[0], ids[1]
    half, _, width = keep.shape
    shift = per.bit_length() - 1
    dims = (((1,), (1,)), ((), ())) if turned else (((1,), (0,)), ((), ()))
    for index, stack in enumerate(stacks):
        total = None
        for number, left in enumerate(lefts):
            part = lax.dot_general(left[...], stack[number], dims, preferred_element_type=WIDE)
            total = part if total is None else total + part
        total = total.astype(LOW)
        base = lax.shift_left(jnp.bitwise_xor(group, index), shift)
        for inside in range(per):
            piece = jnp.bitwise_xor(base + inside, rank)
            held[piece] = total[:, inside * width : (inside + 1) * width]
    keep[...] = held[:half]
    give[...] = held[half:]


def matmul_columns(ids, lefts, offset, rows, stacks, per, ranks, turned, block):
    block = min(block, rows)
    shards = len(stacks)
    width = stacks[0].shape[1 if turned else 2] // per
    first = offset // block
    in_specs = [
        pl.BlockSpec((block, left.shape[1]), lambda i, _: (i + first, 0)) for left in lefts
    ]
    in_specs += [whole(stack.shape) for stack in stacks]
    part = pl.BlockSpec((ranks // 2, block, width), lambda i, _: (0, i, 0))
    shape = jax.ShapeDtypeStruct((ranks // 2, rows, width), LOW)
    size = sum(rows * left.shape[1] * 2 for left in lefts) + 4 * shape.size
    size += sum(stack.size * 2 for stack in stacks)
    flops = 2 * rows * stacks[0].size * shards
    return pl.pallas_call(
        functools.partial(columns_kernel, len(lefts), shards, per, turned),
        grid_spec=pltpu.PrefetchScalarGridSpec(
            num_scalar_prefetch=1,
            grid=(rows // block,),
            in_specs=in_specs,
            out_specs=[part, part],
            scratch_shapes=[pltpu.VMEM((ranks, block, width), LOW)],
        ),
        out_shape=[shape, shape],
        compiler_params=params(),
        cost_estimate=pl.CostEstimate(flops=flops, bytes_accessed=size, transcendentals=0),
    )(ids, *lefts, *stacks)


def tall_kernel(counts, half, wide_left, wide, *refs):
    talls, (keep, give) = refs[: sum(counts)], refs[sum(counts) :]
    results = []
    for count in counts:
        total, offset = None, 0
        for tall in talls[:count]:
            rows = tall.shape[0]
            sides = (wide[0, offset : offset + rows, :], tall[...])
            left, right = sides if wide_left else sides[::-1]
            dims = (((0,), (0,)), ((), ()))
            part = lax.dot_general(left, right, dims, preferred_element_type=WIDE)
            total = part if total is None else total + part
            offset += rows
        talls = talls[count:]
        results.append(total.astype(LOW))

    @pl.when(pl.program_id(0) < half)
    def _():
        for number, result in enumerate(results):
            give[0, number] = result

    @pl.when(pl.program_id(0) >= half)
    def _():
        for number, result in enumerate(results):
            keep[0, number] = result


def matmul_tall(wide, groups, wide_left, block):
    shards, length, features = wide.shape
    columns = groups[0][0].shape[1]
    half = shards // 2
    count = len(groups)
    talls = [tall for group in groups for tall in group]

    def order(i):
        return lax.rem(i + half, shards)

    if wide_left:
        block = min(block, features)
        steps = features // block
        in_specs = [pl.BlockSpec((1, length, block), lambda i, j: (order(i), 0, j))]
        in_specs += [whole(tall.shape) for tall in talls]
        tile = (1, count, block, columns)
        full = (half, count, features, columns)
    else:
        block = min(block, columns)
        steps = columns // block
        in_specs = [pl.BlockSpec((1, length, features), lambda i, j: (order(i), 0, 0))]
        in_specs += [pl.BlockSpec((tall.shape[0], block), lambda i, j: (0, j)) for tall in talls]
        tile = (1, count, block, features)
        full = (half, count, columns, features)

    def give_place(i, j):
        ahead = i < half
        return (jnp.where(ahead, i, half - 1), 0, jnp.where(ahead, j, steps - 1), 0)

    def keep_place(i, j):
        ahead = i < half
        return (jnp.where(ahead, 0, i - half), 0, jnp.where(ahead, 0, j), 0)

    shape = jax.ShapeDtypeStruct(full, LOW)
    size = wide.size * 2 + sum(tall.size * 2 for tall in talls) + 4 * shape.size
    return pl.pallas_call(
        functools.partial(tall_kernel, [len(g) for g in groups], half, wide_left),
        grid=(shards, steps),
        in_specs=in_specs,
        out_specs=[pl.BlockSpec(tile, keep_place), pl.BlockSpec(tile, give_place)],
        out_shape=[shape, shape],
        compiler_params=params(),
        cost_estimate=pl.CostEstimate(
            flops=2 * wide.size * columns * count, bytes_accessed=size, transcendentals=0
        ),
    )(wide, *talls)


def prepare_kernel(scale, query, key, scales, gains, cosine, sine_part, query_low, key_low):
    heads = query.shape[1] // HEAD_DIM
    columns = scales[...].T
    for source, target, number, factor in ((query, query_low, 0, scale), (key, key_low, 1, 1.0)):
        normed = source[...] * columns[:, number : number + 1] * gains[number : number + 1, :]
        for head in range(heads):
            part = normed[:, head * HEAD_DIM : (head + 1) * HEAD_DIM]
            spun = part * cosine[...] + pltpu.roll(part, HEAD_DIM // 2, 1) * sine_part[...]
            target[:, head * HEAD_DIM : (head + 1) * HEAD_DIM] = (spun * factor).astype(LOW)


def prepare(query, key, scales, gains, cosine, sine_part, scale, block):
    length, local = query.shape
    tall = pl.BlockSpec((block, local), lambda i: (i, 0))
    table = pl.BlockSpec((block, HEAD_DIM), lambda i: (i, 0))
    shape = jax.ShapeDtypeStruct((length, local), LOW)
    return pl.pallas_call(
        functools.partial(prepare_kernel, scale),
        grid=(length // block,),
        in_specs=[
            tall,
            tall,
            pl.BlockSpec((8, block), lambda i: (0, i)),
            whole(gains.shape),
            table,
            table,
        ],
        out_specs=[tall, tall],
        out_shape=[shape, shape],
        compiler_params=params(),
        cost_estimate=pl.CostEstimate(
            flops=20 * query.size, bytes_accessed=12 * query.size, transcendentals=0
        ),
    )(query, key, scales, gains, cosine, sine_part)


def unturn_kernel(
    scale, query, key, query_grad, key_grad, scales, gains, cosine, sine_part, *outs
):
    query_hat, key_hat, sums, gain_sums = outs
    heads = query.shape[1] // HEAD_DIM
    columns = scales[...].T
    lines, gain_rows = [], []
    for raw, grad, target, number, factor in (
        (query, query_grad, query_hat, 0, scale),
        (key, key_grad, key_hat, 1, 1.0),
    ):
        for head in range(heads):
            part = slice(head * HEAD_DIM, (head + 1) * HEAD_DIM)
            back = grad[:, part] * factor
            target[:, part] = back * cosine[...] - pltpu.roll(back, HEAD_DIM // 2, 1) * sine_part[...]
        product = target[...] * raw[...]
        gain_rows.append(
            jnp.sum(product * columns[:, number : number + 1], axis=0, keepdims=True)
        )
        weighted = product * gains[number : number + 1, :]
        lines.append(jnp.sum(weighted, axis=1, keepdims=True))
    spread = jnp.concatenate(lines + [jnp.zeros((query.shape[0], 6), WIDE)], axis=1)
    sums[...] = spread.T

    @pl.when(pl.program_id(0) == 0)
    def _():
        gain_sums[...] = jnp.zeros_like(gain_sums)

    for number, line in enumerate(gain_rows):
        gain_sums[number : number + 1, :] += line


def unturn(query, key, query_grad, key_grad, scales, gains, cosine, sine_part, scale, block):
    length, local = query.shape
    tall = pl.BlockSpec((block, local), lambda i: (i, 0))
    table = pl.BlockSpec((block, HEAD_DIM), lambda i: (i, 0))
    line = pl.BlockSpec((8, block), lambda i: (0, i))
    shape = jax.ShapeDtypeStruct((length, local), WIDE)
    return pl.pallas_call(
        functools.partial(unturn_kernel, scale),
        grid=(length // block,),
        in_specs=[tall, tall, tall, tall, line, whole(gains.shape), table, table],
        out_specs=[tall, tall, line, pl.BlockSpec((8, local), lambda i: (0, 0))],
        out_shape=[
            shape,
            shape,
            jax.ShapeDtypeStruct((8, length), WIDE),
            jax.ShapeDtypeStruct((8, local), WIDE),
        ],
        compiler_params=params(),
        cost_estimate=pl.CostEstimate(
            flops=20 * query.size, bytes_accessed=24 * query.size, transcendentals=0
        ),
    )(query, key, query_grad, key_grad, scales, gains, cosine, sine_part)


def query_key_value(results, _, outs):
    query, key, value = results
    outs[0][...] = query
    outs[1][...] = key
    outs[2][...] = value.astype(LOW)


def gated(results, _, outs):
    gate, upward = results
    outs[0][...] = (gate * jax.nn.sigmoid(gate) * upward).astype(LOW)
    outs[1][...] = gate.astype(LOW)
    outs[2][...] = upward.astype(LOW)


def gated_back(results, extras, outs):
    mixed_back = results[0]
    gate = extras[0][...].astype(WIDE)
    upward = extras[1][...].astype(WIDE)
    gate_sig = jax.nn.sigmoid(gate)
    outs[0][...] = (mixed_back * upward * gate_sig * (1.0 + gate * (1.0 - gate_sig))).astype(LOW)
    outs[1][...] = (mixed_back * gate * gate_sig).astype(LOW)


def just_low(results, _, outs):
    outs[0][...] = results[0].astype(LOW)


def per_device(
    layout,
    tokens,
    segment_ids,
    w_query,
    w_key,
    w_value,
    w_out,
    w_gate,
    w_up,
    w_down,
    q_gain,
    k_gain,
    attn_gain,
    ffn_gain,
    out_grad,
):
    seq_len = segment_ids.shape[1]
    rows, local = tokens.shape
    ranks, groups, per = layout.cols, layout.rows, layout.per
    model = local * ranks
    hidden_units = w_gate.shape[1]
    scale = HEAD_DIM ** (-0.5)
    chunks = CHUNKS
    step = rows // chunks
    cuts = [(c * step, (c + 1) * step) for c in range(chunks)]
    row, col = lax.axis_index("rows"), lax.axis_index("cols")
    group = (row // 2) * 2 + col // layout.half
    rank = (row % 2) * layout.half + col % layout.half
    ids = jnp.stack([rank, group]).astype(jnp.int32)
    rank_bits = [1 << i for i in range(ranks.bit_length() - 1)]
    group_bits = [1 << i for i in range(1, groups.bit_length() - 1)]
    cores = rank_bits[-1]

    def links(index):
        return rank_bits[:-1] if index % 2 else rank_bits[:-1][::-1]

    def piece_names(index):
        found = [(0,)]
        for mask in [*links(index), cores]:
            found.append(tuple(j ^ mask for names in found for j in names))
        return found

    far, side = Chain(), Chain()

    def spread(piece, index):
        pieces = [piece[None]]
        for mask in [*links(index), cores]:
            whole_part = pieces[0] if len(pieces) == 1 else jnp.concatenate(pieces)
            pieces.append(send(whole_part, layout.across_ranks(mask)))
        return pieces

    def totals(stacked):
        for mask in rank_bits:
            stacked = stacked + send(stacked, layout.across_ranks(mask))
        return stacked

    def reduce(keep, give, index):
        arrived = send(give, layout.across_ranks(cores))
        names = list(range(cores))
        for mask in links(index + 1):
            total = (keep.astype(WIDE) + arrived.astype(WIDE)).astype(LOW)
            stay = [n for n, name in enumerate(names) if not name & mask]
            leave = [names.index(names[n] ^ mask) for n in stay]
            keep, give = pick(total, stay), pick(total, leave)
            names = [names[n] for n in stay]
            arrived = send(give, layout.across_ranks(mask))
        return keep[0].astype(WIDE) + arrived[0].astype(WIDE)

    def whole_weight(stack):
        found = [far.send(stack, layout.exchange(0)), far.send(stack, layout.exchange(1))]
        for mask in group_bits:
            found += [side.send(v, layout.across_groups(mask)) for v in found]
        return found

    def owners_sum(keep, give):
        for mask in group_bits[::-1]:
            arrived = side.send(give, layout.across_groups(mask))
            total = (keep.astype(WIDE) + arrived.astype(WIDE)).astype(LOW)
            size = total.shape[0] // 2
            keep, give = total[:size], total[size:]
        mine = far.send(keep[0], layout.exchange_back(0))
        other = far.send(give[0], layout.exchange_back(1))
        count = mine.shape[0]
        return [mine[n].astype(WIDE) + other[n].astype(WIDE) for n in range(count)]

    tokens = send(tokens, layout.exchange(0))
    full_qkv = whole_weight(jnp.stack([w_query, w_key, w_value]))
    gains = send(jnp.stack([q_gain, k_gain, attn_gain, ffn_gain]), layout.exchange(0))
    attn_gain, ffn_gain = gains[2], gains[3]
    segment_ids = send(segment_ids, layout.exchange(0))
    full_out = whole_weight(w_out[None])
    full_gated = whole_weight(jnp.stack([w_gate, w_up]))
    full_down = whole_weight(w_down[None])
    out_grad = far.send(out_grad, layout.exchange(0))
    cosine, sine_part = rotation(seq_len, HEAD_DIM)

    made = None
    for index, (low, high) in enumerate(cuts):
        made = matmul_rows(
            ids,
            spread(tokens[low:high], index),
            piece_names(index),
            full_qkv,
            per,
            False,
            query_key_value,
            [],
            [(local, WIDE, True), (local, WIDE, True), (local, LOW, True)],
            (index, chunks, made),
            256,
        )
    query_raw, key_raw, value_low, token_wide = made
    qk_stats = totals(
        jnp.stack([jnp.sum(query_raw * query_raw, axis=1), jnp.sum(key_raw * key_raw, axis=1)])
    )
    scales = jnp.pad(lax.rsqrt(qk_stats / model + EPS), ((0, 6), (0, 0)))
    block = min(512, seq_len)
    query_low, key_low = prepare(
        query_raw, key_raw, scales, gains, cosine, sine_part, scale, block
    )
    names = jnp.arange(DOCUMENTS, dtype=jnp.int32)[:, None]
    before = jnp.sum((segment_ids < names).astype(jnp.int32), axis=1, keepdims=True)
    starts = jnp.sum(jnp.where(segment_ids == names, before, 0), axis=0, keepdims=True)
    lows = starts[0, ::block] // block
    per_chunk = step // block
    columns = functools.partial(matmul_columns, ids, per=per, ranks=ranks, block=256)
    attn_parts, log_totals, out_sums = [], [], []
    for index in range(chunks):
        if index:
            query_low = after(query_low, out_sums[-1])
        out, log_total = attend(
            lows, starts, query_low, key_low, value_low, index * per_chunk, per_chunk, block
        )
        out_sums.append(columns([out], 0, step, full_out, turned=False))
        attn_parts.append(out)
        log_totals.append(log_total)

    def mean_scale(stats):
        return lax.rsqrt(stats / model + EPS)[:, None]

    hidden_made, ffn_made, attn_made = None, None, None
    mixes, gate_backs, up_backs, hidden_cots, layer_outs = [], [], [], [], []
    gain_attn, gain_ffn = 0.0, 0.0
    for index, (low, high) in enumerate(cuts):
        attn_sum = reduce(*out_sums[index], index)
        attn_scale = mean_scale(totals(jnp.sum(attn_sum * attn_sum, axis=1)[None])[0])
        hidden = tokens[low:high].astype(WIDE) + attn_sum * attn_scale * attn_gain
        pieces = spread(hidden.astype(LOW), index)
        if index:
            pieces = after(pieces, forward_last)
        hidden_made = matmul_rows(
            ids,
            pieces,
            piece_names(index),
            full_gated,
            per,
            False,
            gated,
            [],
            [(hidden_units, LOW, False)] * 3,
            (index, chunks, hidden_made),
            256,
        )
        mixed, gate, upward = hidden_made[:3]
        forward_last = columns([mixed], 0, step, full_down, turned=False)
        ffn_sum = reduce(*forward_last, index)
        out_cot = out_grad[low:high].astype(WIDE)
        stats = totals(
            jnp.stack(
                [
                    jnp.sum(ffn_sum * ffn_sum, axis=1),
                    jnp.sum(out_cot * ffn_gain * ffn_sum, axis=1),
                ]
            )
        )
        ffn_scale = mean_scale(stats[0])
        layer_outs.append((hidden + ffn_sum * ffn_scale * ffn_gain).astype(LOW))
        gain_ffn = gain_ffn + jnp.sum(out_cot * ffn_sum * ffn_scale, axis=0)
        ffn_back = norm_back(out_cot, ffn_sum, ffn_scale, ffn_gain, stats[1], model).astype(LOW)
        pieces = spread(ffn_back, index)
        if index:
            pieces = after(pieces, backward_last)
        ffn_made = matmul_rows(
            ids,
            pieces,
            piece_names(index),
            full_down,
            per,
            True,
            gated_back,
            [gate, upward],
            [(hidden_units, LOW, False)] * 2,
            (index, chunks, ffn_made),
            256,
        )
        gate_back, up_back = ffn_made[:2]
        backward_last = columns([gate_back, up_back], 0, step, full_gated, turned=True)
        hidden_cot = out_cot + reduce(*backward_last, index)
        attn_total = totals(jnp.sum(hidden_cot * attn_gain * attn_sum, axis=1)[None])[0]
        gain_attn = gain_attn + jnp.sum(hidden_cot * attn_sum * attn_scale, axis=0)
        attn_back = norm_back(
            hidden_cot, attn_sum, attn_scale, attn_gain, attn_total, model
        ).astype(LOW)
        attn_made = matmul_rows(
            ids,
            spread(attn_back, index),
            piece_names(index),
            full_out,
            per,
            True,
            just_low,
            [],
            [(local, LOW, True)],
            (index, chunks, attn_made),
            256,
        )
        mixes.append(mixed)
        gate_backs.append(gate_back)
        up_backs.append(up_back)
        hidden_cots.append(hidden_cot)

    layer_out = far.send(jnp.concatenate(layer_outs), layout.exchange_back(0))
    grad_down = owners_sum(*matmul_tall(ffn_made[-1], [mixes], False, 512))[0]
    grad_gate, grad_up = owners_sum(
        *matmul_tall(hidden_made[-1], [gate_backs, up_backs], True, 256)
    )
    out_back, attn_wide = attn_made
    grad_out = owners_sum(*matmul_tall(attn_wide, [attn_parts], False, 256))[0]

    query_grad, key_grad, value_grad = attend_back(
        lows,
        starts,
        query_low,
        key_low,
        value_low,
        jnp.concatenate(log_totals, axis=2),
        jnp.concatenate(attn_parts),
        out_back,
        block,
    )
    value_back = value_grad.astype(LOW)
    query_hat, key_hat, sums, gain_sums = unturn(
        query_raw,
        key_raw,
        query_grad,
        key_grad,
        scales,
        gains,
        cosine,
        sine_part,
        scale,
        block,
    )
    qk_totals = totals(sums[:2])
    query_back = norm_back(
        query_hat, query_raw, scales[0][:, None], gains[0], qk_totals[0], model
    ).astype(LOW)
    key_back = norm_back(
        key_hat, key_raw, scales[1][:, None], gains[1], qk_totals[1], model
    ).astype(LOW)

    input_grads = []
    for index, (low, high) in enumerate(cuts):
        total = columns([query_back, key_back, value_back], low, step, full_qkv, turned=True)
        total = reduce(*total, index)
        total = (hidden_cots[index] + total).astype(LOW)
        input_grads.append(send(total, layout.exchange_back(0)))
    grad_query, grad_key, grad_value = owners_sum(
        *matmul_tall(token_wide, [[query_back], [key_back], [value_back]], True, 512)
    )

    gains = jnp.concatenate([gain_sums[:2], gain_attn[None], gain_ffn[None]])
    gains, input_grads[0] = lax.optimization_barrier((gains, input_grads[0]))
    input_grad = jnp.concatenate(input_grads)
    for mask in [1, *group_bits]:
        gains = gains + send(gains, layout.across_groups(mask))
    gains = send(gains, layout.exchange_back(0))
    return (
        layer_out,
        input_grad,
        grad_query,
        grad_key,
        grad_value,
        grad_out,
        grad_gate,
        grad_up,
        grad_down,
        gains[0],
        gains[1],
        gains[2],
        gains[3],
    )


def solution(mesh):
    layout = Layout(mesh.shape["rows"], mesh.shape["cols"])
    both, turned, lone = P("rows", "cols"), P("cols", "rows"), P("cols")
    in_specs = (both, P("rows", None), both, both, both, turned, both, both, turned)
    in_specs += (lone, lone, lone, lone, both)
    out_specs = (both, both, both, both, both, turned, both, both, turned)
    out_specs += (lone, lone, lone, lone)
    return jax.shard_map(
        functools.partial(per_device, layout),
        mesh=mesh,
        in_specs=in_specs,
        out_specs=out_specs,
        check_vma=False,
    )
```

```python
import functools

import jax
import jax.numpy as jnp
from jax import lax
from jax.experimental import pallas as pl
from jax.experimental.pallas import tpu as pltpu
from jax.sharding import PartitionSpec as P

HEAD_DIM = 128
EPS = 1e-06
THETA = 500000.0
MASKED = -1e30
LOW = jnp.bfloat16
WIDE = jnp.float32
CHUNKS = 4
DOCUMENTS = 8
VMEM = 52 * 2**20


def rotation(length, width):
    halfway = width // 2
    rates = THETA ** (-2.0 * jnp.arange(halfway, dtype=WIDE) / width)
    angles = jnp.arange(length, dtype=WIDE)[:, None] * rates[None, :]
    cosine, sine_part = jnp.cos(angles), jnp.sin(angles)
    return (
        jnp.concatenate([cosine, cosine], axis=1),
        jnp.concatenate([-sine_part, sine_part], axis=1),
    )


def attend_kernel(first, block, lows, starts, query, key, value, out, log_total):
    index = pl.program_id(1)
    begin = (first + index) * block
    queries = query[...]
    start = starts[...]
    place = begin + lax.broadcasted_iota(jnp.int32, (1, block), 1)

    def body(step, carry):
        peak, total, held = carry
        rows = pl.ds(pl.multiple_of(step * block, block), block)
        scores = lax.dot_general(
            key[rows, :], queries, (((1,), (1,)), ((), ())), preferred_element_type=WIDE
        )
        key_place = step * block + lax.broadcasted_iota(jnp.int32, (block, 1), 0)
        scores = jnp.where((key_place >= start) & (key_place <= place), scores, MASKED)
        top = jnp.maximum(peak, jnp.max(scores, axis=0, keepdims=True))
        weights = jnp.exp(scores - top)
        fade = jnp.exp(peak - top)
        total = total * fade + jnp.sum(weights, axis=0, keepdims=True)
        held = held * fade + lax.dot_general(
            value[rows, :], weights.astype(LOW), (((0,), (0,)), ((), ())), preferred_element_type=WIDE
        )
        return (top, total, held)

    row = jnp.full((1, block), MASKED, WIDE)
    carry = (row, jnp.zeros((1, block), WIDE), jnp.zeros((HEAD_DIM, block), WIDE))
    peak, total, held = lax.fori_loop(lows[first + index], first + index + 1, body, carry)
    out[...] = (held / total).T.astype(LOW)
    log_total[0] = peak + jnp.log(total)


def attend(lows, starts, query, key, value, first, count, block):
    length, local = query.shape
    heads = local // HEAD_DIM
    rows = count * block
    own = pl.BlockSpec((block, HEAD_DIM), lambda h, i, _: (first + i, h))
    all_keys = pl.BlockSpec((length, HEAD_DIM), lambda h, i, _: (0, h))
    made = pl.BlockSpec((block, HEAD_DIM), lambda h, i, _: (i, h))
    return pl.pallas_call(
        functools.partial(attend_kernel, first, block),
        grid_spec=pltpu.PrefetchScalarGridSpec(
            num_scalar_prefetch=1,
            grid=(heads, count),
            in_specs=[pl.BlockSpec((1, block), lambda h, i, _: (0, first + i)), own, all_keys, all_keys],
            out_specs=[made, pl.BlockSpec((1, 1, block), lambda h, i, _: (h, 0, i))],
        ),
        out_shape=[
            jax.ShapeDtypeStruct((rows, local), LOW),
            jax.ShapeDtypeStruct((heads, 1, rows), WIDE),
        ],
        compiler_params=params(),
        cost_estimate=pl.CostEstimate(
            flops=8 * rows * 1024 * local, bytes_accessed=12 * length * local, transcendentals=0
        ),
    )(lows, starts, query, key, value)


def attend_back_kernel(
    block, lows, starts, query, key, value, log_total, out, grads, dquery, dkey, dvalue
):
    index = pl.program_id(1)
    begin = index * block
    queries, out_grads = query[...], grads[...]
    start = starts[...]
    place = begin + lax.broadcasted_iota(jnp.int32, (1, block), 1)
    lse = log_total[0]
    products = out_grads.astype(WIDE) * out[...].astype(WIDE)
    less = jnp.sum(products.T, axis=0, keepdims=True)

    @pl.when(index == 0)
    def _():
        dkey[...] = jnp.zeros_like(dkey)
        dvalue[...] = jnp.zeros_like(dvalue)

    def body(step, held):
        rows = pl.ds(pl.multiple_of(step * block, block), block)
        keys_here = key[rows, :]
        across = (((1,), (1,)), ((), ()))
        scores = lax.dot_general(keys_here, queries, across, preferred_element_type=WIDE)
        key_place = step * block + lax.broadcasted_iota(jnp.int32, (block, 1), 0)
        allowed = (key_place >= start) & (key_place <= place)
        weights = jnp.exp(jnp.where(allowed, scores - lse, MASKED))
        back = lax.dot_general(value[rows, :], out_grads, across, preferred_element_type=WIDE)
        score_back = (weights * (back - less)).astype(LOW)
        dvalue[rows, :] += jnp.dot(weights.astype(LOW), out_grads, preferred_element_type=WIDE)
        dkey[rows, :] += jnp.dot(score_back, queries, preferred_element_type=WIDE)
        return held + lax.dot_general(
            keys_here, score_back, (((0,), (0,)), ((), ())), preferred_element_type=WIDE
        )

    held = lax.fori_loop(lows[index], index + 1, body, jnp.zeros((HEAD_DIM, block), WIDE))
    dquery[...] = held.T


def attend_back(lows, starts, query, key, value, log_total, out, grads, block):
    length, local = query.shape
    heads = local // HEAD_DIM
    own = pl.BlockSpec((block, HEAD_DIM), lambda h, i, _: (i, h))
    full = pl.BlockSpec((length, HEAD_DIM), lambda h, i, _: (0, h))
    line = pl.BlockSpec((1, 1, block), lambda h, i, _: (h, 0, i))
    shape = jax.ShapeDtypeStruct((length, local), WIDE)
    return pl.pallas_call(
        functools.partial(attend_back_kernel, block),
        grid_spec=pltpu.PrefetchScalarGridSpec(
            num_scalar_prefetch=1,
            grid=(heads, length // block),
            in_specs=[
                pl.BlockSpec((1, block), lambda h, i, _: (0, i)),
                own,
                full,
                full,
                line,
                own,
                own,
            ],
            out_specs=[own, full, full],
        ),
        out_shape=[shape, shape, shape],
        compiler_params=params(),
        cost_estimate=pl.CostEstimate(
            flops=20 * length * 1024 * local, bytes_accessed=20 * length * local, transcendentals=0
        ),
    )(lows, starts, query, key, value, log_total, out, grads)


def norm_back(cot_hat, raw, scale_rows, gain, total, width):
    return scale_rows * (cot_hat * gain) - raw * scale_rows**3 * (total[:, None] / width)


class Layout:
    def __init__(self, rows, cols):
        self.rows, self.cols = rows, cols
        self.half = cols // 2
        self.per = cols // rows

    def name(self, row, col):
        core, x = row & 1, row >> 1
        high, low = col // self.half, col % self.half
        return (x * 2 + high, core * self.half + low)

    def place(self, group, rank):
        x, high = group >> 1, group & 1
        core, low = rank // self.half, rank % self.half
        return (x * 2 + core) * self.cols + high * self.half + low

    def pairs(self, target):
        out = []
        for row in range(self.rows):
            for col in range(self.cols):
                out.append((row * self.cols + col, target(row, col)))
        return out

    def across_ranks(self, mask):
        def target(row, col):
            group, rank = self.name(row, col)
            return self.place(group, rank ^ mask)

        return self.pairs(target)

    def across_groups(self, mask):
        def target(row, col):
            group, rank = self.name(row, col)
            return self.place(group ^ mask, rank)

        return self.pairs(target)

    def exchange(self, flip):
        def target(row, col):
            core, x = row & 1, row >> 1
            high, low = col // self.half, col % self.half
            return (x * 2 + high) * self.cols + (core ^ flip) * self.half + low

        return self.pairs(target)

    def exchange_back(self, flip):
        return [(b, a) for a, b in self.exchange(flip)]


def send(values, pairs):
    return lax.ppermute(values, ("rows", "cols"), pairs)


class Chain:
    def __init__(self):
        self.last = None

    def send(self, values, pairs):
        if self.last is not None:
            values, self.last = lax.optimization_barrier((values, self.last))
        self.last = send(values, pairs)
        return self.last


def pick(values, places):
    if len(places) == 1:
        return values[places[0]][None]
    gap = places[1] - places[0]
    if places == list(range(places[0], places[-1] + 1, gap)):
        return values[places[0] : places[-1] + 1 : gap]
    return jnp.stack([values[p] for p in places])


def after(values, *others):
    return lax.optimization_barrier((values, *others))[0]


def params():
    return pltpu.CompilerParams(vmem_limit_bytes=VMEM)


def whole(shape):
    zeros = (0,) * len(shape)
    return pl.BlockSpec(shape, lambda *_: zeros, pipeline_mode=pl.Buffered(1))


def gather_pieces(ids, pieces, names, wide, per):
    rank, group = ids[0], ids[1]
    width = pieces[0].shape[-1]
    shift = per.bit_length() - 1
    for piece, numbers in zip(pieces, names, strict=True):
        for place, index in enumerate(numbers):
            block = jnp.bitwise_xor(rank, index)
            shard = jnp.bitwise_xor(lax.shift_right_logical(block, shift), group)
            inside = jnp.bitwise_and(block, per - 1)
            columns = pl.ds(pl.multiple_of(inside * width, width), width)
            wide[shard, :, columns] = piece[place]


def dot_rows(wide, shards, turned):
    dims = (((1,), (1,)), ((), ())) if turned else (((1,), (0,)), ((), ()))
    total = None
    for index, shard in enumerate(shards):
        part = lax.dot_general(wide[index], shard, dims, preferred_element_type=WIDE)
        total = part if total is None else total + part
    return total


def rows_kernel(names, count, shards, per, turned, epilogue, extra, merged, ids, *refs):
    pieces, refs = refs[: len(names)], refs[len(names) :]
    stacks, refs = refs[:shards], refs[shards:]
    extras, outs = refs[:extra], refs[extra + merged :]
    wide = outs[-1]
    gather_pieces(ids, pieces, names, wide, per)
    results = [dot_rows(wide, [stack[n] for stack in stacks], turned) for n in range(count)]
    epilogue(results, extras, outs[:-1])


def matmul_rows(ids, pieces, names, stacks, per, turned, epilogue, extras, out_types, into, block):
    rows, width = pieces[0].shape[1:]
    chunk, chunks, earlier = into
    shards = len(stacks)
    count = stacks[0].shape[0]
    block = min(block, rows)
    wide_width = per * width
    first = chunk * (rows // block)

    def tall(columns, merge=False):
        offset = first if merge else 0
        return pl.BlockSpec((block, columns), lambda i, _: (i + offset, 0))

    in_specs = [pl.BlockSpec((p.shape[0], block, width), lambda i, _: (0, i, 0)) for p in pieces]
    in_specs += [whole(stack.shape) for stack in stacks]
    in_specs += [tall(extra.shape[1]) for extra in extras]
    out_specs = [tall(columns, merge) for columns, _, merge in out_types]
    out_specs.append(pl.BlockSpec((shards, block, wide_width), lambda i, _: (0, i + first, 0)))
    out_shape = [
        jax.ShapeDtypeStruct((rows * chunks if merge else rows, columns), kind)
        for columns, kind, merge in out_types
    ]
    out_shape.append(jax.ShapeDtypeStruct((shards, rows * chunks, wide_width), LOW))
    merged = [i for i, kind in enumerate(out_types) if kind[2]] + [len(out_types)]
    handed = [] if earlier is None else [earlier[i] for i in merged]
    in_specs += [pl.BlockSpec(memory_space=pl.ANY) for _ in handed]
    operands = [ids, *pieces, *stacks, *extras]
    aliases = {len(operands) + n: i for n, i in enumerate(merged)} if handed else {}
    body = functools.partial(
        rows_kernel, names, count, shards, per, turned, epilogue, len(extras), len(handed)
    )
    size = sum(a.size * a.dtype.itemsize for a in operands)
    size += sum(columns * rows * jnp.dtype(kind).itemsize for columns, kind, _ in out_types)
    flops = 2 * rows * stacks[0].size * shards
    return pl.pallas_call(
        body,
        grid_spec=pltpu.PrefetchScalarGridSpec(
            num_scalar_prefetch=1,
            grid=(rows // block,),
            in_specs=in_specs,
            out_specs=out_specs,
        ),
        out_shape=out_shape,
        input_output_aliases=aliases,
        compiler_params=params(),
        cost_estimate=pl.CostEstimate(flops=flops, bytes_accessed=size, transcendentals=0),
    )(*operands, *handed)


def columns_kernel(count, shards, per, turned, ids, *refs):
    lefts, stacks = refs[:count], refs[count : count + shards]
    keep, give, held = refs[count + shards :]
    rank, group = ids[0], ids[1]
    half, _, width = keep.shape
    shift = per.bit_length() - 1
    dims = (((1,), (1,)), ((), ())) if turned else (((1,), (0,)), ((), ()))
    for index, stack in enumerate(stacks):
        total = None
        for number, left in enumerate(lefts):
            part = lax.dot_general(left[...], stack[number], dims, preferred_element_type=WIDE)
            total = part if total is None else total + part
        total = total.astype(LOW)
        base = lax.shift_left(jnp.bitwise_xor(group, index), shift)
        for inside in range(per):
            piece = jnp.bitwise_xor(base + inside, rank)
            held[piece] = total[:, inside * width : (inside + 1) * width]
    keep[...] = held[:half]
    give[...] = held[half:]


def matmul_columns(ids, lefts, offset, rows, stacks, per, ranks, turned, block):
    block = min(block, rows)
    shards = len(stacks)
    width = stacks[0].shape[1 if turned else 2] // per
    first = offset // block
    in_specs = [
        pl.BlockSpec((block, left.shape[1]), lambda i, _: (i + first, 0)) for left in lefts
    ]
    in_specs += [whole(stack.shape) for stack in stacks]
    part = pl.BlockSpec((ranks // 2, block, width), lambda i, _: (0, i, 0))
    shape = jax.ShapeDtypeStruct((ranks // 2, rows, width), LOW)
    size = sum(rows * left.shape[1] * 2 for left in lefts) + 4 * shape.size
    size += sum(stack.size * 2 for stack in stacks)
    flops = 2 * rows * stacks[0].size * shards
    return pl.pallas_call(
        functools.partial(columns_kernel, len(lefts), shards, per, turned),
        grid_spec=pltpu.PrefetchScalarGridSpec(
            num_scalar_prefetch=1,
            grid=(rows // block,),
            in_specs=in_specs,
            out_specs=[part, part],
            scratch_shapes=[pltpu.VMEM((ranks, block, width), LOW)],
        ),
        out_shape=[shape, shape],
        compiler_params=params(),
        cost_estimate=pl.CostEstimate(flops=flops, bytes_accessed=size, transcendentals=0),
    )(ids, *lefts, *stacks)


def tall_kernel(counts, half, wide_left, wide, *refs):
    talls, (keep, give) = refs[: sum(counts)], refs[sum(counts) :]
    results = []
    for count in counts:
        total, offset = None, 0
        for tall in talls[:count]:
            rows = tall.shape[0]
            sides = (wide[0, offset : offset + rows, :], tall[...])
            left, right = sides if wide_left else sides[::-1]
            dims = (((0,), (0,)), ((), ()))
            part = lax.dot_general(left, right, dims, preferred_element_type=WIDE)
            total = part if total is None else total + part
            offset += rows
        talls = talls[count:]
        results.append(total.astype(LOW))

    @pl.when(pl.program_id(0) < half)
    def _():
        for number, result in enumerate(results):
            give[0, number] = result

    @pl.when(pl.program_id(0) >= half)
    def _():
        for number, result in enumerate(results):
            keep[0, number] = result


def matmul_tall(wide, groups, wide_left, block):
    shards, length, features = wide.shape
    columns = groups[0][0].shape[1]
    half = shards // 2
    count = len(groups)
    talls = [tall for group in groups for tall in group]

    def order(i):
        return lax.rem(i + half, shards)

    if wide_left:
        block = min(block, features)
        steps = features // block
        in_specs = [pl.BlockSpec((1, length, block), lambda i, j: (order(i), 0, j))]
        in_specs += [whole(tall.shape) for tall in talls]
        tile = (1, count, block, columns)
        full = (half, count, features, columns)
    else:
        block = min(block, columns)
        steps = columns // block
        in_specs = [pl.BlockSpec((1, length, features), lambda i, j: (order(i), 0, 0))]
        in_specs += [pl.BlockSpec((tall.shape[0], block), lambda i, j: (0, j)) for tall in talls]
        tile = (1, count, block, features)
        full = (half, count, columns, features)

    def give_place(i, j):
        ahead = i < half
        return (jnp.where(ahead, i, half - 1), 0, jnp.where(ahead, j, steps - 1), 0)

    def keep_place(i, j):
        ahead = i < half
        return (jnp.where(ahead, 0, i - half), 0, jnp.where(ahead, 0, j), 0)

    shape = jax.ShapeDtypeStruct(full, LOW)
    size = wide.size * 2 + sum(tall.size * 2 for tall in talls) + 4 * shape.size
    return pl.pallas_call(
        functools.partial(tall_kernel, [len(g) for g in groups], half, wide_left),
        grid=(shards, steps),
        in_specs=in_specs,
        out_specs=[pl.BlockSpec(tile, keep_place), pl.BlockSpec(tile, give_place)],
        out_shape=[shape, shape],
        compiler_params=params(),
        cost_estimate=pl.CostEstimate(
            flops=2 * wide.size * columns * count, bytes_accessed=size, transcendentals=0
        ),
    )(wide, *talls)


def prepare_kernel(scale, query, key, scales, gains, cosine, sine_part, query_low, key_low):
    heads = query.shape[1] // HEAD_DIM
    columns = scales[...].T
    for source, target, number, factor in ((query, query_low, 0, scale), (key, key_low, 1, 1.0)):
        normed = source[...] * columns[:, number : number + 1] * gains[number : number + 1, :]
        for head in range(heads):
            part = normed[:, head * HEAD_DIM : (head + 1) * HEAD_DIM]
            spun = part * cosine[...] + pltpu.roll(part, HEAD_DIM // 2, 1) * sine_part[...]
            target[:, head * HEAD_DIM : (head + 1) * HEAD_DIM] = (spun * factor).astype(LOW)


def prepare(query, key, scales, gains, cosine, sine_part, scale, block):
    length, local = query.shape
    tall = pl.BlockSpec((block, local), lambda i: (i, 0))
    table = pl.BlockSpec((block, HEAD_DIM), lambda i: (i, 0))
    shape = jax.ShapeDtypeStruct((length, local), LOW)
    return pl.pallas_call(
        functools.partial(prepare_kernel, scale),
        grid=(length // block,),
        in_specs=[
            tall,
            tall,
            pl.BlockSpec((8, block), lambda i: (0, i)),
            whole(gains.shape),
            table,
            table,
        ],
        out_specs=[tall, tall],
        out_shape=[shape, shape],
        compiler_params=params(),
        cost_estimate=pl.CostEstimate(
            flops=20 * query.size, bytes_accessed=12 * query.size, transcendentals=0
        ),
    )(query, key, scales, gains, cosine, sine_part)


def unturn_kernel(
    scale, query, key, query_grad, key_grad, scales, gains, cosine, sine_part, *outs
):
    query_hat, key_hat, sums, gain_sums = outs
    heads = query.shape[1] // HEAD_DIM
    columns = scales[...].T
    lines, gain_rows = [], []
    for raw, grad, target, number, factor in (
        (query, query_grad, query_hat, 0, scale),
        (key, key_grad, key_hat, 1, 1.0),
    ):
        for head in range(heads):
            part = slice(head * HEAD_DIM, (head + 1) * HEAD_DIM)
            back = grad[:, part] * factor
            target[:, part] = back * cosine[...] - pltpu.roll(back, HEAD_DIM // 2, 1) * sine_part[...]
        product = target[...] * raw[...]
        gain_rows.append(
            jnp.sum(product * columns[:, number : number + 1], axis=0, keepdims=True)
        )
        weighted = product * gains[number : number + 1, :]
        lines.append(jnp.sum(weighted, axis=1, keepdims=True))
    spread = jnp.concatenate(lines + [jnp.zeros((query.shape[0], 6), WIDE)], axis=1)
    sums[...] = spread.T

    @pl.when(pl.program_id(0) == 0)
    def _():
        gain_sums[...] = jnp.zeros_like(gain_sums)

    for number, line in enumerate(gain_rows):
        gain_sums[number : number + 1, :] += line


def unturn(query, key, query_grad, key_grad, scales, gains, cosine, sine_part, scale, block):
    length, local = query.shape
    tall = pl.BlockSpec((block, local), lambda i: (i, 0))
    table = pl.BlockSpec((block, HEAD_DIM), lambda i: (i, 0))
    line = pl.BlockSpec((8, block), lambda i: (0, i))
    shape = jax.ShapeDtypeStruct((length, local), WIDE)
    return pl.pallas_call(
        functools.partial(unturn_kernel, scale),
        grid=(length // block,),
        in_specs=[tall, tall, tall, tall, line, whole(gains.shape), table, table],
        out_specs=[tall, tall, line, pl.BlockSpec((8, local), lambda i: (0, 0))],
        out_shape=[
            shape,
            shape,
            jax.ShapeDtypeStruct((8, length), WIDE),
            jax.ShapeDtypeStruct((8, local), WIDE),
        ],
        compiler_params=params(),
        cost_estimate=pl.CostEstimate(
            flops=20 * query.size, bytes_accessed=24 * query.size, transcendentals=0
        ),
    )(query, key, query_grad, key_grad, scales, gains, cosine, sine_part)


def query_key_value(results, _, outs):
    query, key, value = results
    outs[0][...] = query
    outs[1][...] = key
    outs[2][...] = value.astype(LOW)


def gated(results, _, outs):
    gate, upward = results
    outs[0][...] = (gate * jax.nn.sigmoid(gate) * upward).astype(LOW)
    outs[1][...] = gate.astype(LOW)
    outs[2][...] = upward.astype(LOW)


def gated_back(results, extras, outs):
    mixed_back = results[0]
    gate = extras[0][...].astype(WIDE)
    upward = extras[1][...].astype(WIDE)
    gate_sig = jax.nn.sigmoid(gate)
    outs[0][...] = (mixed_back * upward * gate_sig * (1.0 + gate * (1.0 - gate_sig))).astype(LOW)
    outs[1][...] = (mixed_back * gate * gate_sig).astype(LOW)


def just_low(results, _, outs):
    outs[0][...] = results[0].astype(LOW)


def per_device(
    layout,
    tokens,
    segment_ids,
    w_query,
    w_key,
    w_value,
    w_out,
    w_gate,
    w_up,
    w_down,
    q_gain,
    k_gain,
    attn_gain,
    ffn_gain,
    out_grad,
):
    seq_len = segment_ids.shape[1]
    rows, local = tokens.shape
    ranks, groups, per = layout.cols, layout.rows, layout.per
    model = local * ranks
    hidden_units = w_gate.shape[1]
    scale = HEAD_DIM ** (-0.5)
    chunks = CHUNKS
    step = rows // chunks
    cuts = [(c * step, (c + 1) * step) for c in range(chunks)]
    row, col = lax.axis_index("rows"), lax.axis_index("cols")
    group = (row // 2) * 2 + col // layout.half
    rank = (row % 2) * layout.half + col % layout.half
    ids = jnp.stack([rank, group]).astype(jnp.int32)
    rank_bits = [1 << i for i in range(ranks.bit_length() - 1)]
    group_bits = [1 << i for i in range(1, groups.bit_length() - 1)]
    cores = rank_bits[-1]

    def links(index):
        return rank_bits[:-1] if index % 2 else rank_bits[:-1][::-1]

    def piece_names(index):
        found = [(0,)]
        for mask in [*links(index), cores]:
            found.append(tuple(j ^ mask for names in found for j in names))
        return found

    far, side = Chain(), Chain()

    def spread(piece, index):
        pieces = [piece[None]]
        for mask in [*links(index), cores]:
            whole_part = pieces[0] if len(pieces) == 1 else jnp.concatenate(pieces)
            pieces.append(send(whole_part, layout.across_ranks(mask)))
        return pieces

    def totals(stacked):
        for mask in rank_bits:
            stacked = stacked + send(stacked, layout.across_ranks(mask))
        return stacked

    def reduce(keep, give, index):
        arrived = send(give, layout.across_ranks(cores))
        names = list(range(cores))
        for mask in links(index + 1):
            total = (keep.astype(WIDE) + arrived.astype(WIDE)).astype(LOW)
            stay = [n for n, name in enumerate(names) if not name & mask]
            leave = [names.index(names[n] ^ mask) for n in stay]
            keep, give = pick(total, stay), pick(total, leave)
            names = [names[n] for n in stay]
            arrived = send(give, layout.across_ranks(mask))
        return keep[0].astype(WIDE) + arrived[0].astype(WIDE)

    def whole_weight(stack):
        found = [far.send(stack, layout.exchange(0)), far.send(stack, layout.exchange(1))]
        for mask in group_bits:
            found += [side.send(v, layout.across_groups(mask)) for v in found]
        return found

    def owners_sum(keep, give):
        for mask in group_bits[::-1]:
            arrived = side.send(give, layout.across_groups(mask))
            total = (keep.astype(WIDE) + arrived.astype(WIDE)).astype(LOW)
            size = total.shape[0] // 2
            keep, give = total[:size], total[size:]
        mine = far.send(keep[0], layout.exchange_back(0))
        other = far.send(give[0], layout.exchange_back(1))
        count = mine.shape[0]
        return [mine[n].astype(WIDE) + other[n].astype(WIDE) for n in range(count)]

    tokens = send(tokens, layout.exchange(0))
    full_qkv = whole_weight(jnp.stack([w_query, w_key, w_value]))
    gains = send(jnp.stack([q_gain, k_gain, attn_gain, ffn_gain]), layout.exchange(0))
    attn_gain, ffn_gain = gains[2], gains[3]
    segment_ids = send(segment_ids, layout.exchange(0))
    full_out = whole_weight(w_out[None])
    full_gated = whole_weight(jnp.stack([w_gate, w_up]))
    full_down = whole_weight(w_down[None])
    out_grad = far.send(out_grad, layout.exchange(0))
    cosine, sine_part = rotation(seq_len, HEAD_DIM)

    made = None
    for index, (low, high) in enumerate(cuts):
        made = matmul_rows(
            ids,
            spread(tokens[low:high], index),
            piece_names(index),
            full_qkv,
            per,
            False,
            query_key_value,
            [],
            [(local, WIDE, True), (local, WIDE, True), (local, LOW, True)],
            (index, chunks, made),
            256,
        )
    query_raw, key_raw, value_low, token_wide = made
    qk_stats = totals(
        jnp.stack([jnp.sum(query_raw * query_raw, axis=1), jnp.sum(key_raw * key_raw, axis=1)])
    )
    scales = jnp.pad(lax.rsqrt(qk_stats / model + EPS), ((0, 6), (0, 0)))
    block = min(512, seq_len)
    query_low, key_low = prepare(
        query_raw, key_raw, scales, gains, cosine, sine_part, scale, block
    )
    names = jnp.arange(DOCUMENTS, dtype=jnp.int32)[:, None]
    before = jnp.sum((segment_ids < names).astype(jnp.int32), axis=1, keepdims=True)
    starts = jnp.sum(jnp.where(segment_ids == names, before, 0), axis=0, keepdims=True)
    lows = starts[0, ::block] // block
    per_chunk = step // block
    columns = functools.partial(matmul_columns, ids, per=per, ranks=ranks, block=256)
    attn_parts, log_totals, out_sums = [], [], []
    for index in range(chunks):
        if index:
            query_low = after(query_low, out_sums[-1])
        out, log_total = attend(
            lows, starts, query_low, key_low, value_low, index * per_chunk, per_chunk, block
        )
        out_sums.append(columns([out], 0, step, full_out, turned=False))
        attn_parts.append(out)
        log_totals.append(log_total)

    def mean_scale(stats):
        return lax.rsqrt(stats / model + EPS)[:, None]

    hidden_made, ffn_made, attn_made = None, None, None
    mixes, gate_backs, up_backs, hidden_cots, layer_outs = [], [], [], [], []
    gain_attn, gain_ffn = 0.0, 0.0
    for index, (low, high) in enumerate(cuts):
        attn_sum = reduce(*out_sums[index], index)
        attn_scale = mean_scale(totals(jnp.sum(attn_sum * attn_sum, axis=1)[None])[0])
        hidden = tokens[low:high].astype(WIDE) + attn_sum * attn_scale * attn_gain
        pieces = spread(hidden.astype(LOW), index)
        if index:
            pieces = after(pieces, forward_last)
        hidden_made = matmul_rows(
            ids,
            pieces,
            piece_names(index),
            full_gated,
            per,
            False,
            gated,
            [],
            [(hidden_units, LOW, False)] * 3,
            (index, chunks, hidden_made),
            256,
        )
        mixed, gate, upward = hidden_made[:3]
        forward_last = columns([mixed], 0, step, full_down, turned=False)
        ffn_sum = reduce(*forward_last, index)
        out_cot = out_grad[low:high].astype(WIDE)
        stats = totals(
            jnp.stack(
                [
                    jnp.sum(ffn_sum * ffn_sum, axis=1),
                    jnp.sum(out_cot * ffn_gain * ffn_sum, axis=1),
                ]
            )
        )
        ffn_scale = mean_scale(stats[0])
        layer_outs.append((hidden + ffn_sum * ffn_scale * ffn_gain).astype(LOW))
        gain_ffn = gain_ffn + jnp.sum(out_cot * ffn_sum * ffn_scale, axis=0)
        ffn_back = norm_back(out_cot, ffn_sum, ffn_scale, ffn_gain, stats[1], model).astype(LOW)
        pieces = spread(ffn_back, index)
        if index:
            pieces = after(pieces, backward_last)
        ffn_made = matmul_rows(
            ids,
            pieces,
            piece_names(index),
            full_down,
            per,
            True,
            gated_back,
            [gate, upward],
            [(hidden_units, LOW, False)] * 2,
            (index, chunks, ffn_made),
            256,
        )
        gate_back, up_back = ffn_made[:2]
        backward_last = columns([gate_back, up_back], 0, step, full_gated, turned=True)
        hidden_cot = out_cot + reduce(*backward_last, index)
        attn_total = totals(jnp.sum(hidden_cot * attn_gain * attn_sum, axis=1)[None])[0]
        gain_attn = gain_attn + jnp.sum(hidden_cot * attn_sum * attn_scale, axis=0)
        attn_back = norm_back(
            hidden_cot, attn_sum, attn_scale, attn_gain, attn_total, model
        ).astype(LOW)
        attn_made = matmul_rows(
            ids,
            spread(attn_back, index),
            piece_names(index),
            full_out,
            per,
            True,
            just_low,
            [],
            [(local, LOW, True)],
            (index, chunks, attn_made),
            256,
        )
        mixes.append(mixed)
        gate_backs.append(gate_back)
        up_backs.append(up_back)
        hidden_cots.append(hidden_cot)

    layer_out = far.send(jnp.concatenate(layer_outs), layout.exchange_back(0))
    grad_down = owners_sum(*matmul_tall(ffn_made[-1], [mixes], False, 1024))[0]
    grad_gate, grad_up = owners_sum(
        *matmul_tall(hidden_made[-1], [gate_backs, up_backs], True, 512)
    )
    out_back, attn_wide = attn_made
    grad_out = owners_sum(*matmul_tall(attn_wide, [attn_parts], False, 256))[0]

    query_grad, key_grad, value_grad = attend_back(
        lows,
        starts,
        query_low,
        key_low,
        value_low,
        jnp.concatenate(log_totals, axis=2),
        jnp.concatenate(attn_parts),
        out_back,
        block,
    )
    value_back = value_grad.astype(LOW)
    query_hat, key_hat, sums, gain_sums = unturn(
        query_raw,
        key_raw,
        query_grad,
        key_grad,
        scales,
        gains,
        cosine,
        sine_part,
        scale,
        block,
    )
    qk_totals = totals(sums[:2])
    query_back = norm_back(
        query_hat, query_raw, scales[0][:, None], gains[0], qk_totals[0], model
    ).astype(LOW)
    key_back = norm_back(
        key_hat, key_raw, scales[1][:, None], gains[1], qk_totals[1], model
    ).astype(LOW)

    input_grads = []
    for index, (low, high) in enumerate(cuts):
        total = columns([query_back, key_back, value_back], low, step, full_qkv, turned=True)
        total = reduce(*total, index)
        total = (hidden_cots[index] + total).astype(LOW)
        input_grads.append(send(total, layout.exchange_back(0)))
    grad_query, grad_key, grad_value = owners_sum(
        *matmul_tall(token_wide, [[query_back], [key_back], [value_back]], True, 512)
    )

    gains = jnp.concatenate([gain_sums[:2], gain_attn[None], gain_ffn[None]])
    gains, input_grads[0] = lax.optimization_barrier((gains, input_grads[0]))
    input_grad = jnp.concatenate(input_grads)
    for mask in [1, *group_bits]:
        gains = gains + send(gains, layout.across_groups(mask))
    gains = send(gains, layout.exchange_back(0))
    return (
        layer_out,
        input_grad,
        grad_query,
        grad_key,
        grad_value,
        grad_out,
        grad_gate,
        grad_up,
        grad_down,
        gains[0],
        gains[1],
        gains[2],
        gains[3],
    )


def solution(mesh):
    layout = Layout(mesh.shape["rows"], mesh.shape["cols"])
    both, turned, lone = P("rows", "cols"), P("cols", "rows"), P("cols")
    in_specs = (both, P("rows", None), both, both, both, turned, both, both, turned)
    in_specs += (lone, lone, lone, lone, both)
    out_specs = (both, both, both, both, both, turned, both, both, turned)
    out_specs += (lone, lone, lone, lone)
    return jax.shard_map(
        functools.partial(per_device, layout),
        mesh=mesh,
        in_specs=in_specs,
        out_specs=out_specs,
        check_vma=False,
    )
```
